256 devices in a mesh: dp: 32 (over x, z_hi, core), mp: 8 (over y, z_lo).
Axes of the slice: x: 4, y: 4, z: 8 (z_hi: 4, z_lo: 2; z = z_hi * 2 + z_lo), core: 2. Of those that a mesh axis runs over, the one named last changes fastest.
Arguments:
- grads: bfloat16 [32, 48, 512, 512], P('dp', None, 'mp'), may hold values from -0.046875 to 0.046875
- owners: int32 [48, 1], replicated, may hold values from 0 to 31; in each aligned block of 48 rows (0 to 47, 48 to 95, ...) at most 4 rows name the same one
- left_stat: float32 [32, 4, 512, 512], P('dp', None, 'mp'), as said below
- right_stat: float32 [32, 4, 512, 512], P('dp', None, 'mp'), as said below
- first_moment: float32 [32, 4, 512, 512], P('dp', None, 'mp'), may hold values from -0.3 to 0.3
- second_moment: float32 [32, 4, 512, 512], P('dp', None, 'mp'), may hold values from 0.0001 to 0.01
Outputs:
- direction: bfloat16 [48, 512, 512], P(None, 'mp')
- left_out: float32 [32, 4, 512, 512], P('dp', None, 'mp')
- right_out: float32 [32, 4, 512, 512], P('dp', None, 'mp')
- first_out: float32 [32, 4, 512, 512], P('dp', None, 'mp')
- second_out: float32 [32, 4, 512, 512], P('dp', None, 'mp')
The draws below stay inside these ranges and needn't reach their ends.
Inputs may be any that keep to these rules, and one draw needn't show every extreme that they name: `owners`: no owner holds more than 4 blocks, some owner holds exactly 4, and every owner holds at least one. `left_stat`: each slot's matrix is symmetric positive definite. `right_stat`: each slot's matrix is symmetric positive definite.
All inputs are finite; a program needn't handle non-finite values.
Results may differ from the reference program's by a relative error of at most 0.025.
Values may be sent and summed in bfloat16 or wider, within the bound.
A program may use at most 128 MiB of HBM per device.

```python
import math
import jax
import jax.numpy as jnp
import numpy as np
from jax import lax

B = 512
ITERS = 6
MOST = 4
NB = 48
N_DP = 32


def definite_draw(key):

    def one_owner(owner_key):
        normals = jax.random.normal(owner_key, (MOST, B, 2 * B), jnp.float32)
        matrices = jnp.einsum('sik,sjk->sij', normals, normals, precision=lax.Precision.HIGHEST) / (2.0 * B)
        return matrices
    owner_keys = jax.random.split(key, N_DP)
    return lax.map(one_owner, owner_keys)


def draw_left_stat(key, part):
    return definite_draw(jax.random.fold_in(key, 11))


def draw_right_stat(key, part):
    return definite_draw(jax.random.fold_in(key, 23))


def shard_levels(stream_key, shape, shards, smallest, high):
    loudness, own = 1.0, jax.random.fold_in(stream_key, 6)
    for dim, parts in shards:
        draws = jnp.exp(jax.random.uniform(jax.random.fold_in(own, dim), (parts,), jnp.float32, smallest / len(shards), high / len(shards)))
        loudness = loudness * jnp.repeat(draws, shape[dim] // parts).reshape([-1 if axis == dim else 1 for axis in range(len(shape))])
    return loudness


def deal_out(rng, own, number, rows, number_of, top, limit, skew):
    sequence = jax.random.permutation(rng, number_of)
    heavy_load, ordinary = portions_of(number_of, rows * top, limit, skew, True), portions_of(number_of, rows * top, limit, skew, False)
    places = jnp.arange(number_of)

    def named(tallies, offset_by):
        used = int((tallies > 0).sum())
        fixed = max(1, used // 4)
        passed = fixed + (places - fixed + offset_by * (used - fixed)) % max(1, number_of - fixed)
        return jnp.zeros((number_of,), jnp.int32).at[sequence[jnp.where(places < fixed, places, passed)]].set(jnp.asarray(tallies, jnp.int32))

    tallies = jnp.where(number % 4 == 0, named(heavy_load, number // 4), named(ordinary, number - number // 4 - 1))
    mixed = jax.random.permutation(jax.random.fold_in(own, 3), number_of)
    giver, taker = mixed[0:number_of // 2 * 2:2], mixed[1:number_of // 2 * 2:2]
    room = jnp.minimum(tallies[giver] - 1, limit - tallies[taker]) // 2
    room = jnp.where((giver == sequence[0]) | (taker == sequence[0]) | (tallies[taker] == 0), 0, jnp.maximum(room, 0))
    passed = jax.random.randint(jax.random.fold_in(own, 4), (number_of // 2,), 0, 1 << 20) % (room + 1)
    tallies = tallies.at[giver].add(-passed).at[taker].add(passed)
    labels = jnp.searchsorted(jnp.cumsum(tallies), jnp.arange(rows * top), side="right").astype(jnp.int32)
    table = labels.reshape(top, rows).T
    table = table[jax.random.permutation(jax.random.fold_in(own, 1), rows)]
    offset_by = jax.random.randint(jax.random.fold_in(own, 2), (rows, 1), 0, top)
    return jnp.take_along_axis(table, (jnp.arange(top)[None, :] + offset_by) % top, axis=1)


def portions_of(count, total, reach, slope, full):
    weights = [(1 << 20) // math.isqrt(grade ** slope) + 1 for grade in range(1, count + 1)]
    largest = reach if full else min(reach, max(-(-total // count), total * weights[0] // sum(weights)))
    least = 1 if total - largest >= count - 1 else 0
    holding, surplus = [largest] + [least] * (count - 1), total - largest - least * (count - 1)
    while surplus > 0:
        free = [i for i in range(1, count) if holding[i] < largest] or [i for i in range(1, count) if holding[i] < reach]
        whole, left = sum([weights[i] for i in free]), surplus
        for i in free:
            extra = min(reach - holding[i], max(1, left * weights[i] // whole), surplus)
            holding[i] = holding[i] + extra
            surplus = surplus - extra
    return np.array(holding)


def normal_values(own_key, extent, width, bound, cuts=(), kind=jnp.bfloat16):
    factor_of = shard_levels(own_key, extent, cuts, -0.22, 0.18) if cuts else 1.0
    drawn = jax.random.normal(own_key, extent, jnp.float32) * width * factor_of
    return jnp.minimum(jnp.maximum(drawn, -bound), bound).astype(kind)


def setup_inputs(seed: int = 0) -> dict:
    key_of = jax.random.split(jax.random.key(seed), 7)
    grads = normal_values(key_of[0], (N_DP, NB, B, B), (N_DP * B) ** -0.5, 0.046875, ((0, 32), (2, 8)))
    owners_keys = jax.random.split(jax.random.fold_in(key_of[1], 1), NB // NB)
    owners_turns = jax.random.permutation(jax.random.fold_in(key_of[1], 3), NB // NB)
    owners = jax.vmap(lambda own, number: deal_out(jax.random.fold_in(key_of[1], 2), own, number, NB, N_DP, 1, MOST, 2))(owners_keys, owners_turns).reshape((NB, 1))
    left_stat = draw_left_stat(jax.random.fold_in(key_of[6], 71), 0)
    right_stat = draw_right_stat(jax.random.fold_in(key_of[6], 71), 0)
    first_moment = normal_values(key_of[4], (N_DP, MOST, B, B), 0.05, 0.3, ((0, 32), (2, 8)), jnp.float32)
    second_moment = jnp.clip(jnp.exp(math.log(0.01) - 4.6051702 * jax.random.uniform(key_of[5], (N_DP, MOST, B, B), jnp.float32) ** shard_levels(key_of[5], (N_DP, MOST, B, B), ((0, 32), (2, 8)), -0.2, 0.2)), 0.0001, 0.01)
    return {"grads": grads, "owners": owners, "left_stat": left_stat, "right_stat": right_stat, "first_moment": first_moment, "second_moment": second_moment}


HIGHEST_PRECISION = lax.Precision.HIGHEST

def matmul(left, right):
    return jnp.matmul(left.astype(jnp.float32), right.astype(jnp.float32), precision=HIGHEST_PRECISION)

def inverse_root(matrix):
    order_size = matrix.shape[-1]
    identity = jnp.eye(order_size, dtype=jnp.float32)
    frobenius = jnp.sqrt(jnp.sum(matrix * matrix))
    scaling = 5.0 / (2.0 * frobenius)
    current = (scaling * matrix).astype(jnp.bfloat16)
    root_now = (identity * scaling ** 0.25).astype(jnp.bfloat16)
    for sweep in range(ITERS):
        factor_now = ((5.0 * identity - current.astype(jnp.float32)) / 4.0).astype(jnp.bfloat16)
        root_now = matmul(root_now, factor_now).astype(jnp.bfloat16)
        power_now = matmul(factor_now, factor_now).astype(jnp.bfloat16)
        power_now = matmul(power_now, factor_now).astype(jnp.bfloat16)
        power_now = matmul(power_now, factor_now).astype(jnp.bfloat16)
        current = matmul(power_now, current).astype(jnp.bfloat16)
    return root_now

def block_step(items):
    summed_grad, left_old, right_old, first_old, second_old = items
    rounded = summed_grad.astype(jnp.bfloat16)
    left_new = 0.9 * left_old + 0.1 * matmul(rounded, rounded.T)
    right_new = 0.9 * right_old + 0.1 * matmul(rounded.T, rounded)
    left_root = inverse_root(left_new)
    right_root = inverse_root(right_new)
    left_half = matmul(left_root, rounded).astype(jnp.bfloat16)
    shampoo = matmul(left_half, right_root)
    first_new = 0.9 * first_old + 0.1 * summed_grad
    second_new = 0.95 * second_old + 0.05 * summed_grad * summed_grad
    adam_step = first_new / (jnp.sqrt(second_new) + 1e-08)
    adam_rows = jnp.sqrt(lax.optimization_barrier(jnp.sum(adam_step * adam_step, axis=1, keepdims=True)))
    shampoo_rows = jnp.sqrt(lax.optimization_barrier(jnp.sum(shampoo * shampoo, axis=1, keepdims=True))) + 1e-06
    direction = (shampoo * (adam_rows / shampoo_rows)).astype(jnp.bfloat16)
    return (direction, left_new, right_new, first_new, second_new)

def reference(grads, owners, left_stat, right_stat, first_moment, second_moment):
    owner_of = owners[:, 0].astype(jnp.int32)
    same_owner = (owner_of[:, None] == owner_of[None, :]).astype(jnp.int32)
    positions = jnp.arange(NB, dtype=jnp.int32)
    earlier = (positions[None, :] < positions[:, None]).astype(jnp.int32)
    slot_of = lax.optimization_barrier(jnp.sum(same_owner * earlier, axis=1)).astype(jnp.int32)
    summed = lax.optimization_barrier(jnp.sum(grads.astype(jnp.float32), axis=0))
    items = (summed, left_stat[owner_of, slot_of], right_stat[owner_of, slot_of], first_moment[owner_of, slot_of], second_moment[owner_of, slot_of])
    direction, left_new, right_new, first_new, second_new = lax.map(block_step, items)
    left_out = left_stat.at[owner_of, slot_of].set(left_new)
    right_out = right_stat.at[owner_of, slot_of].set(right_new)
    first_out = first_moment.at[owner_of, slot_of].set(first_new)
    second_out = second_moment.at[owner_of, slot_of].set(second_new)
    return (direction, left_out, right_out, first_out, second_out)
```

```python
import jax
import jax.numpy as jnp
from jax import lax
from jax.experimental import pallas as pl
from jax.experimental.pallas import tpu as pltpu
from jax.sharding import PartitionSpec as P

ITERS = 6
MESH = pl.DeviceIdType.MESH
VMEM = pl.BlockSpec(memory_space=pltpu.VMEM)
SMEM = pl.BlockSpec(memory_space=pltpu.SMEM)
F32, BF16 = jnp.float32, jnp.bfloat16
NX, NZ, NC, NM = 4, 4, 2, 8
NK = NX * NZ
ROWS, COLS, HALF = 64, 512, 32
SLOTS = 4
BLOCKS = 48
OWNERS = NK * NC
EXTRAS = BLOCKS - OWNERS
FAR_FIRST = (2, 1, 3)


def place():
    me = lax.axis_index("dp")
    return me // (NZ * NC), (me // NC) % NZ, me % NC, lax.axis_index("mp")


def dp_of(x, z, c):
    return {"dp": (x * NZ + z) * NC + c}


def remote(src, dst, send, recv, device):
    copy = pltpu.make_async_remote_copy(
        src_ref=src, dst_ref=dst, send_sem=send, recv_sem=recv, device_id=device, device_id_type=MESH
    )
    copy.start()
    return copy


def greet(devices):
    barrier = pltpu.get_barrier_semaphore()
    for device in devices:
        pl.semaphore_signal(barrier, inc=1, device_id=device, device_id_type=MESH)
    pl.semaphore_wait(barrier, len(devices))


def dp_peers(x, z, c):
    return (
        [dp_of(x, z, 1 - c)]
        + [dp_of((x + k) % NX, z, c) for k in (1, 2, 3)]
        + [dp_of(x, (z + k) % NZ, c) for k in (1, 2, 3)]
    )


def mp_peers(j):
    return [{"mp": (j + k) % NM} for k in range(1, NM)]


def total(*parts):
    value = parts[0].astype(F32)
    for part in parts[1:]:
        value = value + part.astype(F32)
    return value.astype(BF16)


def spread_extras(ext, x, z, c, sz, rz, sx, rx, sc, rc):
    half = pl.ds(c * HALF, HALF)
    mine = ext.at[x * NZ + z, half]
    zs = [remote(mine, mine, sz.at[k - 1], rz.at[k - 1], dp_of(x, (z + k) % NZ, c)) for k in FAR_FIRST]
    for copy in zs:
        copy.wait_recv()
    line = ext.at[pl.ds(x * NZ, NZ), half]
    xs = [remote(line, line, sx.at[k - 1], rx.at[k - 1], dp_of((x + k) % NX, z, c)) for k in FAR_FIRST]
    cs = [remote(line, line, sc.at[0], rc.at[0], dp_of(x, z, 1 - c))]
    for k in (1, 3, 2):
        [copy] = [copy for copy, at in zip(xs, FAR_FIRST) if at == k]
        copy.wait_recv()
        came = ext.at[pl.ds(((x + NX - k) % NX) * NZ, NZ), half]
        cs.append(remote(came, came, sc.at[k], rc.at[k], dp_of(x, z, 1 - c)))
    return zs + xs, cs


def reduce_kernel(
    order, extra_of, grads, left_stat, right_stat, own, stat,
    send_f, send_e, recv_f, recv_e, acc_f, acc_e, from_x_f, from_z_f, from_x_e, from_z_e, sum_f, sum_e, ext,
    s_stat, r_stat, s_cf, r_cf, s_ce, r_ce, s_xf, r_xf, s_zf, r_zf, s_xe, r_xe, s_ze, r_ze,
    s_gz, r_gz, s_gx, r_gx, s_gc, r_gc,
):
    x, z, c, j = place()
    other = 1 - c
    greet(dp_peers(x, z, c) + mp_peers(j))

    for k in range(NK):
        send_e[k] = grads[order[OWNERS + k], pl.ds(other * HALF, HALF)]
    core_e = remote(send_e, recv_e, s_ce.at[0], r_ce.at[0], dp_of(x, z, other))
    core_f = []
    for step, k in enumerate((2, 1, 3, 0)):
        to = (x + k) % NX
        for q in range(NZ):
            send_f[to * NZ + q] = grads[order[(to * NZ + q) * NC + other]]
        rows = pl.ds(to * NZ, NZ)
        core_f.append(
            remote(send_f.at[rows], recv_f.at[rows], s_cf.at[step], r_cf.at[step], dp_of(x, z, other))
        )

    stat_rows = pl.ds(j * ROWS, ROWS)
    stats = []
    for k in range(1, NM):
        to = (j + k) % NM
        make = lambda source: pltpu.make_async_remote_copy(
            src_ref=source.at[to // 2], dst_ref=stat.at[stat_rows], send_sem=s_stat.at[k - 1],
            recv_sem=r_stat.at[k - 1], device_id={"mp": to}, device_id_type=MESH,
        )

        @pl.when(to % 2 == c)
        def _():
            make(left_stat).start()

        @pl.when(to % 2 != c)
        def _():
            make(right_stat).start()

        stats.append(make(left_stat))

    @pl.when(j % 2 == c)
    def _():
        stat[stat_rows] = left_stat[j // 2]

    @pl.when(j % 2 != c)
    def _():
        stat[stat_rows] = right_stat[j // 2]

    core_e.wait_recv()
    for k in range(NK):
        acc_e[k % NZ, k // NZ] = total(grads[order[OWNERS + k], pl.ds(c * HALF, HALF)], recv_e[k])
    z_e = []
    for k in FAR_FIRST:
        to = (z + k) % NZ
        z_e.append(remote(acc_e.at[to], from_z_e.at[k - 1], s_ze.at[k - 1], r_ze.at[k - 1], dp_of(x, to, c)))
    x_f = []
    for step, k in enumerate((2, 1, 3, 0)):
        to = (x + k) % NX
        core_f[step].wait_recv()
        for q in range(NZ):
            at = to * NZ + q
            acc_f[at] = total(grads[order[at * NC + c]], recv_f[at])
        if k:
            rows = pl.ds(to * NZ, NZ)
            x_f.append(
                remote(acc_f.at[rows], from_x_f.at[k - 1], s_xf.at[k - 1], r_xf.at[k - 1], dp_of(to, z, c))
            )
    for copy in z_e:
        copy.wait_recv()
    for q in range(NX):
        sum_e[q] = total(acc_e[z, q], from_z_e[0, q], from_z_e[1, q], from_z_e[2, q])
    x_e = []
    for k in FAR_FIRST:
        to = (x + k) % NX
        x_e.append(remote(sum_e.at[to], from_x_e.at[k - 1], s_xe.at[k - 1], r_xe.at[k - 1], dp_of(to, z, c)))
    for copy in x_f:
        copy.wait_recv()
    for q in range(NZ):
        sum_f[q] = total(acc_f[x * NZ + q], from_x_f[0, q], from_x_f[1, q], from_x_f[2, q])
    z_f = []
    for k in FAR_FIRST:
        to = (z + k) % NZ
        z_f.append(remote(sum_f.at[to], from_z_f.at[k - 1], s_zf.at[k - 1], r_zf.at[k - 1], dp_of(x, to, c)))
    for copy in x_e:
        copy.wait_recv()
    ext[x * NZ + z, pl.ds(c * HALF, HALF)] = total(sum_e[x], from_x_e[0], from_x_e[1], from_x_e[2])
    spread, cores = spread_extras(ext, x, z, c, s_gz, r_gz, s_gx, r_gx, s_gc, r_gc)
    for copy in z_f:
        copy.wait_recv()
    own[0] = total(sum_f[z], from_z_f[0], from_z_f[1], from_z_f[2])
    for copy in cores:
        copy.wait_recv()
    for s in range(1, SLOTS):
        own[s] = ext[extra_of[s]]
    for copy in stats:
        copy.wait()
    for copy in [core_e] + core_f + z_e + x_f + x_e + z_f + spread + cores:
        copy.wait_send()


def reduced(order, extra_of, grads, left_stat, right_stat):
    dma = pltpu.SemaphoreType.DMA
    pairs = [NM - 1, NX, 1, 3, 3, 3, 3, 3, 3, NX]
    return pl.pallas_call(
        reduce_kernel,
        out_shape=(
            jax.ShapeDtypeStruct((SLOTS, ROWS, COLS), BF16),
            jax.ShapeDtypeStruct((NM * ROWS, COLS), F32),
        ),
        in_specs=[SMEM, SMEM, VMEM, VMEM, VMEM],
        out_specs=(VMEM, VMEM),
        scratch_shapes=[
            pltpu.VMEM((NK, ROWS, COLS), BF16),
            pltpu.VMEM((NK, HALF, COLS), BF16),
            pltpu.VMEM((NK, ROWS, COLS), BF16),
            pltpu.VMEM((NK, HALF, COLS), BF16),
            pltpu.VMEM((NK, ROWS, COLS), BF16),
            pltpu.VMEM((NZ, NX, HALF, COLS), BF16),
            pltpu.VMEM((3, NZ, ROWS, COLS), BF16),
            pltpu.VMEM((3, ROWS, COLS), BF16),
            pltpu.VMEM((3, HALF, COLS), BF16),
            pltpu.VMEM((3, NX, HALF, COLS), BF16),
            pltpu.VMEM((NZ, ROWS, COLS), BF16),
            pltpu.VMEM((NX, HALF, COLS), BF16),
            pltpu.VMEM((EXTRAS, ROWS, COLS), BF16),
        ]
        + [dma((n,)) for n in pairs for _ in range(2)],
        compiler_params=pltpu.CompilerParams(
            collective_id=0, has_side_effects=True, vmem_limit_bytes=40 << 20
        ),
        name="reduce_grads",
    )(order, extra_of, grads, left_stat, right_stat)


def mm(a, b):
    return jnp.dot(a, b, preferred_element_type=F32)


def root_kernel(
    own, stat, first, second, terms, update,
    grad, norms, norms_in, mat, term, power, factor, current, root, half, half_in, turned,
    s_g, r_g, s_n, r_n, s_t, r_t, s_h, r_h, s_d, r_d,
):
    _, _, c, j = place()
    slot = j // 2
    side = (j + c) % 2
    partner = {"mp": j + 1 - 2 * (j % 2)}
    greet(mp_peers(j))
    my_rows = pl.ds(j * ROWS, ROWS)
    order = NM * ROWS

    g_copies = []
    for k in (4, 3, 5, 2, 6, 1, 7):
        to = (j + k) % NM
        g_copies.append(
            remote(own.at[to // 2], grad.at[my_rows], s_g.at[k - 1], r_g.at[k - 1], {"mp": to})
        )
    grad[my_rows] = own[slot]
    for s in range(SLOTS):
        g = own[s].astype(F32)
        m = 0.9 * first[s] + 0.1 * g
        v = 0.95 * second[s] + 0.05 * g * g
        a = m / (jnp.sqrt(v) + 1e-8)
        norms[s] = jnp.broadcast_to(jnp.sqrt(jnp.sum(a * a, axis=1, keepdims=True)), (ROWS, 128))
    norms_in[my_rows] = norms[slot]
    for copy in g_copies:
        copy.wait_recv()
    n_copies = []
    for k in range(1, NM):
        to = (j + k) % NM
        n_copies.append(
            remote(norms.at[to // 2], norms_in.at[my_rows], s_n.at[k - 1], r_n.at[k - 1], {"mp": to})
        )

    @pl.when(side == 0)
    def _():
        g = grad[...]
        mat[...] = lax.dot_general(g, g, (((1,), (1,)), ((), ())), preferred_element_type=F32)

    @pl.when(side == 1)
    def _():
        g = grad[...]
        mat[...] = lax.dot_general(g, g, (((0,), (0,)), ((), ())), preferred_element_type=F32)

    product = mat[...]
    term[...] = product.astype(BF16)
    whole = 0.9 * stat[...] + 0.1 * product
    mat[...] = whole
    t_copies = []
    for k in range(1, NM):
        to = (j + k) % NM
        t_copies.append(
            remote(
                term.at[pl.ds(to * ROWS, ROWS)], terms.at[side, slot], s_t.at[k - 1], r_t.at[j], {"mp": to}
            )
        )
    terms[side, slot] = term[my_rows]

    frobenius = jnp.sqrt(jnp.sum(whole * whole, keepdims=True))
    scaling = 5.0 / (2.0 * frobenius)
    start = jnp.sqrt(jnp.sqrt(scaling)).astype(BF16).astype(F32)
    diagonal = lax.broadcasted_iota(jnp.int32, (order, order), 0) == lax.broadcasted_iota(
        jnp.int32, (order, order), 1
    )
    five = jnp.where(diagonal, 5.0, 0.0).astype(F32)
    current[...] = (scaling * mat[...]).astype(BF16)
    factor[...] = ((five - current[...].astype(F32)) * 0.25).astype(BF16)
    root[...] = (start * factor[...].astype(F32)).astype(BF16)

    def sweep(_, carry):
        power[...] = mm(factor[...], factor[...]).astype(BF16)
        power[...] = mm(power[...], power[...]).astype(BF16)
        current[...] = mm(power[...], current[...]).astype(BF16)
        factor[...] = ((five - current[...].astype(F32)) * 0.25).astype(BF16)
        root[...] = mm(root[...], factor[...]).astype(BF16)
        return carry

    lax.fori_loop(0, ITERS - 1, sweep, 0)

    step = 2 * ROWS
    h_copies = []
    for i in range(order // step):
        rows = pl.ds(i * step, step)
        h_copies.append(
            pltpu.make_async_remote_copy(
                src_ref=half.at[rows], dst_ref=half_in.at[rows], send_sem=s_h.at[i], recv_sem=r_h.at[i],
                device_id=partner, device_id_type=MESH,
            )
        )
    d_copies = []
    for to in range(NM):
        d_copies.append(
            pltpu.make_async_remote_copy(
                src_ref=turned.at[pl.ds(to * ROWS, ROWS)], dst_ref=update.at[slot], send_sem=s_d.at[to],
                recv_sem=r_d.at[slot], device_id={"mp": to}, device_id_type=MESH,
            )
        )
    for k in range(1, NM):
        n_copies[k - 1].wait_recv()

    @pl.when(side == 0)
    def _():
        for i in range(order // step):
            rows = pl.ds(i * step, step)
            half[rows] = mm(root[rows], grad[...]).astype(BF16)
            h_copies[i].start()
        for copy in h_copies:
            copy.wait_send()

    @pl.when(side == 1)
    def _():
        for i in range(order // step):
            rows = pl.ds(i * step, step)
            h_copies[i].wait_recv()
            s = mm(half_in[rows], root[...])
            length = jnp.sqrt(jnp.sum(s * s, axis=1, keepdims=True)) + 1e-6
            turned[rows] = (s * (norms_in[rows, 0:1] / length)).astype(BF16)
            for to in (2 * i, 2 * i + 1):

                @pl.when(j != to)
                def _():
                    d_copies[to].start()

                @pl.when(j == to)
                def _():
                    update[slot] = turned[pl.ds(to * ROWS, ROWS)]

        for to in range(NM):

            @pl.when(j != to)
            def _():
                d_copies[to].wait_send()

    for s in range(SLOTS):

        @pl.when(j != 2 * s + 1 - c)
        def _():
            pltpu.make_async_remote_copy(
                src_ref=turned.at[pl.ds(0, ROWS)], dst_ref=update.at[s], send_sem=s_d.at[0],
                recv_sem=r_d.at[s], device_id=partner, device_id_type=MESH,
            ).wait_recv()

    for i in range(NM):

        @pl.when(j != i)
        def _():
            pltpu.make_async_remote_copy(
                src_ref=term.at[pl.ds(0, ROWS)], dst_ref=terms.at[(i + c) % 2, i // 2], send_sem=s_t.at[0],
                recv_sem=r_t.at[i], device_id=partner, device_id_type=MESH,
            ).wait_recv()

    for copy in g_copies + n_copies + t_copies:
        copy.wait_send()


def rooted(own, stat, first, second):
    dma = pltpu.SemaphoreType.DMA
    order = NM * ROWS
    square = lambda kind: pltpu.VMEM((order, COLS), kind)
    pairs = [NM - 1, NM - 1, None, order // (2 * ROWS), None]
    sems = [
        dma((NM - 1,)), dma((NM - 1,)), dma((NM - 1,)), dma((NM - 1,)), dma((NM - 1,)), dma((NM,)),
        dma((4,)), dma((4,)), dma((NM,)), dma((SLOTS,)),
    ]
    return pl.pallas_call(
        root_kernel,
        out_shape=(
            jax.ShapeDtypeStruct((2, SLOTS, ROWS, COLS), BF16),
            jax.ShapeDtypeStruct((SLOTS, ROWS, COLS), BF16),
        ),
        in_specs=[VMEM] * 4,
        out_specs=(VMEM, VMEM),
        scratch_shapes=[
            square(BF16),
            pltpu.VMEM((SLOTS, ROWS, 128), F32),
            pltpu.VMEM((order, 128), F32),
            square(F32),
        ]
        + [square(BF16)] * 8
        + sems,
        compiler_params=pltpu.CompilerParams(
            collective_id=1, has_side_effects=True, vmem_limit_bytes=40 << 20
        ),
        name="inverse_roots",
    )(own, stat, first, second)


def share_kernel(
    mine_of, place_of, update, out,
    all_of, send_e, recv_e, acc_e, from_x, from_z, sum_e,
    s_ce, r_ce, s_xe, r_xe, s_ze, r_ze, s_gz, r_gz, s_gx, r_gx, s_gc, r_gc, s_fz, r_fz, s_fx, r_fx, s_fc, r_fc,
):
    x, z, c, _ = place()
    other = 1 - c
    greet(dp_peers(x, z, c))
    me = c * NK + x * NZ + z
    all_of[me] = update[0]

    def picked(e, which):
        at = mine_of[e]
        kept = jnp.where(at > 0, 1.0, 0.0).astype(F32)
        value = update[at, pl.ds(which * HALF, HALF)].astype(F32)
        return jnp.where(jnp.full(value.shape, kept) > 0.5, value, 0.0)

    for e in range(EXTRAS):
        send_e[e] = picked(e, other).astype(BF16)
    core_e = remote(send_e, recv_e, s_ce.at[0], r_ce.at[0], dp_of(x, z, other))
    mine = all_of.at[me]
    f_z = [
        remote(mine, mine, s_fz.at[k - 1], r_fz.at[k - 1], dp_of(x, (z + k) % NZ, c)) for k in FAR_FIRST
    ]
    core_e.wait_recv()
    x_e = []
    for k in (2, 1, 3, 0):
        to = (x + k) % NX
        for q in range(NZ):
            e = to * NZ + q
            acc_e[e] = (picked(e, c) + recv_e[e].astype(F32)).astype(BF16)
        if k:
            rows = pl.ds(to * NZ, NZ)
            x_e.append(
                remote(acc_e.at[rows], from_x.at[k - 1], s_xe.at[k - 1], r_xe.at[k - 1], dp_of(to, z, c))
            )
    for copy in f_z:
        copy.wait_recv()
    line = all_of.at[pl.ds(c * NK + x * NZ, NZ)]
    f_x = [
        remote(line, line, s_fx.at[k - 1], r_fx.at[k - 1], dp_of((x + k) % NX, z, c)) for k in FAR_FIRST
    ]
    f_c = [remote(line, line, s_fc.at[0], r_fc.at[0], dp_of(x, z, other))]
    for copy in x_e:
        copy.wait_recv()
    for q in range(NZ):
        sum_e[q] = total(acc_e[x * NZ + q], from_x[0, q], from_x[1, q], from_x[2, q])
    z_e = []
    for k in FAR_FIRST:
        to = (z + k) % NZ
        z_e.append(remote(sum_e.at[to], from_z.at[k - 1], s_ze.at[k - 1], r_ze.at[k - 1], dp_of(x, to, c)))
    for copy in z_e:
        copy.wait_recv()
    all_of[OWNERS + x * NZ + z, pl.ds(c * HALF, HALF)] = total(sum_e[z], from_z[0], from_z[1], from_z[2])
    ext = all_of.at[pl.ds(OWNERS, EXTRAS)]
    spread, cores = spread_extras(ext, x, z, c, s_gz, r_gz, s_gx, r_gx, s_gc, r_gc)
    for k in (1, 3, 2):
        [copy] = [copy for copy, at in zip(f_x, FAR_FIRST) if at == k]
        copy.wait_recv()
        came = all_of.at[pl.ds(c * NK + ((x + NX - k) % NX) * NZ, NZ)]
        f_c.append(remote(came, came, s_fc.at[k], r_fc.at[k], dp_of(x, z, other)))
    for copy in f_c + cores:
        copy.wait_recv()
    for b in range(BLOCKS):
        out[b] = all_of[place_of[b]]
    for copy in [core_e] + f_z + x_e + f_x + z_e + spread + f_c + cores:
        copy.wait_send()


def shared(mine_of, place_of, update):
    dma = pltpu.SemaphoreType.DMA
    pairs = [1, 3, 3, 3, 3, NX, 3, 3, NX]
    return pl.pallas_call(
        share_kernel,
        out_shape=jax.ShapeDtypeStruct((BLOCKS, ROWS, COLS), BF16),
        in_specs=[SMEM, SMEM, VMEM],
        out_specs=VMEM,
        scratch_shapes=[
            pltpu.VMEM((BLOCKS, ROWS, COLS), BF16),
            pltpu.VMEM((EXTRAS, HALF, COLS), BF16),
            pltpu.VMEM((EXTRAS, HALF, COLS), BF16),
            pltpu.VMEM((EXTRAS, HALF, COLS), BF16),
            pltpu.VMEM((3, NZ, HALF, COLS), BF16),
            pltpu.VMEM((3, HALF, COLS), BF16),
            pltpu.VMEM((NZ, HALF, COLS), BF16),
        ]
        + [dma((n,)) for n in pairs for _ in range(2)],
        compiler_params=pltpu.CompilerParams(
            collective_id=2, has_side_effects=True, vmem_limit_bytes=40 << 20
        ),
        name="share_directions",
    )(mine_of, place_of, update)


def tables(owners):
    owner = owners[:, 0]
    me = lax.axis_index("dp")
    spots = jnp.arange(BLOCKS, dtype=jnp.int32)
    earlier = spots[None, :] < spots[:, None]
    slot = jnp.sum((owner[:, None] == owner[None, :]) & earlier, axis=1, dtype=jnp.int32)
    again = slot > 0
    rank = jnp.sum(again[None, :] & earlier, axis=1, dtype=jnp.int32)
    sorted_at = jnp.where(again, OWNERS + rank, owner)
    order = jnp.sum(jnp.where(sorted_at[None, :] == spots[:, None], spots[None, :], 0), axis=1)
    place_of = jnp.where(again, OWNERS + rank, (owner % NC) * NK + owner // NC)
    mine = owner == me
    slots = jnp.arange(SLOTS, dtype=jnp.int32)
    holds = mine[None, :] & (slot[None, :] == slots[:, None])
    occupied = jnp.any(holds, axis=1)
    extra_of = jnp.sum(jnp.where(holds & again[None, :], rank[None, :], 0), axis=1)
    extras = jnp.arange(EXTRAS, dtype=jnp.int32)
    held = (mine & again)[None, :] & (rank[None, :] == extras[:, None])
    mine_of = jnp.sum(jnp.where(held, slot[None, :], 0), axis=1)
    return order, place_of, occupied, extra_of, mine_of


def body(grads, owners, left_stat, right_stat, first_moment, second_moment):
    order, place_of, occupied, extra_of, mine_of = tables(owners)
    left, right, first, second = left_stat[0], right_stat[0], first_moment[0], second_moment[0]
    own, stat = reduced(order, extra_of, grads[0], left, right)
    terms, update = rooted(own, stat, first, second)
    direction = shared(mine_of, place_of, update)
    mask = occupied[:, None, None]
    summed = own.astype(F32)
    left_out = jnp.where(mask, 0.9 * left + 0.1 * terms[0].astype(F32), left)[None]
    right_out = jnp.where(mask, 0.9 * right + 0.1 * terms[1].astype(F32), right)[None]
    first_out = jnp.where(mask, 0.9 * first + 0.1 * summed, first)[None]
    second_out = jnp.where(mask, 0.95 * second + 0.05 * summed * summed, second)[None]
    return direction, left_out, right_out, first_out, second_out


def solution(mesh):
    split = P("dp", None, "mp", None)
    return jax.shard_map(
        body,
        mesh=mesh,
        in_specs=(split, P(), split, split, split, split),
        out_specs=(P(None, "mp", None), split, split, split, split),
        check_vma=False,
    )
```

```python
import jax
import jax.numpy as jnp
from jax import lax
from jax.experimental import pallas as pl
from jax.experimental.pallas import tpu as pltpu
from jax.sharding import PartitionSpec as P

ITERS = 6
MESH = pl.DeviceIdType.MESH
VMEM = pl.BlockSpec(memory_space=pltpu.VMEM)
SMEM = pl.BlockSpec(memory_space=pltpu.SMEM)
ANY = pl.BlockSpec(memory_space=pl.ANY)
F32, BF16 = jnp.float32, jnp.bfloat16
NX, NZ, NC, NM = 4, 4, 2, 8
NK = NX * NZ
ROWS, COLS, HALF = 64, 512, 32
ORDER = NM * ROWS
SLOTS = 4
BLOCKS = 48
OWNERS = NK * NC
EXTRAS = BLOCKS - OWNERS
FAR_FIRST = (2, 1, 3)
SEMS = 192


def dp_of(x, z, c):
    return {"dp": (x * NZ + z) * NC + c}


def device_of(x, z, c, j):
    return {"dp": (x * NZ + z) * NC + c, "mp": j}


def total(*parts):
    value = parts[0].astype(F32)
    for part in parts[1:]:
        value = value + part.astype(F32)
    return value.astype(BF16)


def mm(a, b):
    return jnp.dot(a, b, preferred_element_type=F32)


class Wires:
    def __init__(self, send, recv):
        self.send, self.recv, self.used, self.sent = send, recv, 0, []

    def take(self, count):
        self.used += count
        assert self.used <= SEMS
        return self.used - count

    def make(self, src, dst, device, at_send, at_recv):
        return pltpu.make_async_remote_copy(
            src_ref=src, dst_ref=dst, send_sem=self.send.at[at_send], recv_sem=self.recv.at[at_recv],
            device_id=device, device_id_type=MESH,
        )

    def go(self, src, dst, device):
        at = self.take(1)
        copy = self.make(src, dst, device, at, at)
        copy.start()
        self.sent.append(copy)
        return copy


class RingReduce:
    def __init__(self, wires, acc, passed, came, x, to):
        self.wires, self.acc, self.passed, self.came, self.x, self.to = wires, acc, passed, came, x, to
        self.right, self.left, self.far = (x + 1) % NX, (x + 3) % NX, (x + 2) % NX

    def part(self, at, h):
        return self.acc.at[pl.ds(at * NZ + 2 * h, 2)]

    def send_far(self):
        self.a = self.wires.go(self.part(self.far, 0), self.passed.at[0], self.to(self.right))
        self.b = self.wires.go(self.part(self.far, 1), self.passed.at[1], self.to(self.left))

    def send_right(self):
        self.c = self.wires.go(self.part(self.right, 1), self.came.at[0, pl.ds(2, 2)], self.to(self.right))

    def send_left(self):
        self.d = self.wires.go(self.part(self.left, 0), self.came.at[1, pl.ds(0, 2)], self.to(self.left))

    def forward(self):
        self.a.wait_recv()
        for q in range(2):
            at = self.right * NZ + q
            self.acc[at] = total(self.acc[at], self.passed[0, q])
        self.e = self.wires.go(self.part(self.right, 0), self.came.at[0, pl.ds(0, 2)], self.to(self.right))
        self.b.wait_recv()
        for q in range(2):
            at = self.left * NZ + 2 + q
            self.acc[at] = total(self.acc[at], self.passed[1, q])
        self.f = self.wires.go(self.part(self.left, 1), self.came.at[1, pl.ds(2, 2)], self.to(self.left))

    def finish(self, out):
        for copy in (self.c, self.d, self.e, self.f):
            copy.wait_recv()
        for q in range(NZ):
            out[q] = total(self.acc[self.x * NZ + q], self.came[0, q], self.came[1, q])


class RingGather:
    def __init__(self, wires, part, x, to):
        self.wires, self.part = wires, part
        self.x, self.right, self.left = x, (x + 1) % NX, (x + 3) % NX
        self.to_right, self.to_left = to(self.right), to(self.left)

    def push(self, at, h, device):
        return self.wires.go(self.part(at, h), self.part(at, h), device)

    def start(self):
        self.a = self.push(self.x, 0, self.to_right)
        self.b = self.push(self.x, 1, self.to_left)
        self.c = self.push(self.x, 1, self.to_right)
        self.d = self.push(self.x, 0, self.to_left)

    def forward(self):
        self.a.wait_recv()
        self.e = self.push(self.left, 0, self.to_right)
        self.b.wait_recv()
        self.f = self.push(self.right, 1, self.to_left)

    def finish_near(self):
        self.c.wait_recv()
        self.d.wait_recv()

    def finish_far(self):
        self.e.wait_recv()
        self.f.wait_recv()


def kernel(
    order, place_of, occupied, extra_of, mine_of, grads, left, right, first, second,
    out, left_out, right_out, first_out, second_out,
    gv, lv, rv, fv, sv,
    send_f, send_e, recv_f, recv_e, acc_f, acc_e, pass_f, pass_e, came_f, came_e, sum_f, sum_e,
    from_z_f, from_z_e, ext, own,
    grad, stat, norms, norms_in, mat, term, terms, power, factor, current, root, half, half_in, turned, update,
    all_of, send_d, recv_d, acc_d, pass_d, came_d, sum_d, from_z_d,
    send_sem, recv_sem, load_sem, stat_sem,
):
    me = lax.axis_index("dp")
    j = lax.axis_index("mp")
    x, z, c = me // (NZ * NC), (me // NC) % NZ, me % NC
    y, zl = j // 2, j % 2
    other = 1 - c
    core = dp_of(x, z, other)
    to_x = lambda at: dp_of(at, z, c)
    w = Wires(send_sem, recv_sem)
    my_rows = pl.ds(j * ROWS, ROWS)
    lanes = lax.broadcasted_iota(jnp.int32, (ROWS, 128), 1)
    lines = lax.broadcasted_iota(jnp.int32, (ROWS, 128), 0)

    loads = [
        pltpu.make_async_copy(src, dst, load_sem.at[i])
        for i, (src, dst) in enumerate(((grads, gv), (left, lv), (right, rv), (first, fv), (second, sv)))
    ]
    for copy in loads:
        copy.start()

    barrier = pltpu.get_barrier_semaphore()
    greeted = 0
    for k in range(1, 4):
        for device in (dp_of((x + k) % NX, z, c), dp_of(x, (z + k) % NZ, c)):
            pl.semaphore_signal(barrier, inc=1, device_id=device, device_id_type=MESH)
            greeted += 1
    for k in range(NM):
        for which in range(NC):
            if k or which:
                device = device_of(x, z, (c + which) % NC, (j + k) % NM)
                pl.semaphore_signal(barrier, inc=1, device_id=device, device_id_type=MESH)
                greeted += 1
    pl.semaphore_wait(barrier, greeted)

    loads[0].wait()
    for k in range(NK):
        send_e[k] = gv[order[OWNERS + k], pl.ds(other * HALF, HALF)]
    core_e = w.go(send_e, recv_e, core)
    turns = (2, 1, 3, 0)
    core_f = []
    for k in turns:
        at = (x + k) % NX
        for q in range(NZ):
            send_f[at * NZ + q] = gv[order[(at * NZ + q) * NC + other]]
        rows = pl.ds(at * NZ, NZ)
        core_f.append(w.go(send_f.at[rows], recv_f.at[rows], core))

    loads[1].wait()
    loads[2].wait()
    stat_send, stat_recv = w.take(2 * SLOTS), w.take(NM)
    stat_copies = []
    for s in range(SLOTS):
        for role, source in enumerate((lv, rv)):
            copy = w.make(
                source.at[s], stat.at[my_rows], device_of(x, z, role, 2 * s + c), stat_send + 2 * s + role,
                stat_recv + j,
            )
            here = (c == role) & (j == 2 * s + c)
            stat_copies.append((here, copy))

            @pl.when(jnp.logical_not(here))
            def _():
                copy.start()

            @pl.when(here)
            def _():
                stat[my_rows] = source[s]

    ring_e = RingReduce(w, acc_e, pass_e, came_e, x, to_x)
    ring_f = RingReduce(w, acc_f, pass_f, came_f, x, to_x)
    core_e.wait_recv()
    for k in range(NK):
        acc_e[k] = total(gv[order[OWNERS + k], pl.ds(c * HALF, HALF)], recv_e[k])
    ring_e.send_far()
    ring_e.send_right()
    ring_e.send_left()

    def add_f(step):
        at = (x + turns[step]) % NX
        core_f[step].wait_recv()
        for q in range(NZ):
            acc_f[at * NZ + q] = total(gv[order[(at * NZ + q) * NC + c]], recv_f[at * NZ + q])

    add_f(0)
    ring_f.send_far()
    add_f(1)
    ring_f.send_right()
    ring_e.forward()
    add_f(2)
    ring_f.send_left()
    add_f(3)
    ring_e.finish(sum_e)
    z_e = [w.go(sum_e.at[(z + k) % NZ], from_z_e.at[k - 1], dp_of(x, (z + k) % NZ, c)) for k in FAR_FIRST]
    ring_f.forward()
    for copy in z_e:
        copy.wait_recv()
    mine = ext.at[x * NZ + z, pl.ds(c * HALF, HALF)]
    ext[x * NZ + z, pl.ds(c * HALF, HALF)] = total(sum_e[z], from_z_e[0], from_z_e[1], from_z_e[2])
    z_g = [w.go(mine, mine, dp_of(x, (z + k) % NZ, c)) for k in FAR_FIRST]
    ring_f.finish(sum_f)
    z_f = [w.go(sum_f.at[(z + k) % NZ], from_z_f.at[k - 1], dp_of(x, (z + k) % NZ, c)) for k in FAR_FIRST]
    for copy in z_g:
        copy.wait_recv()

    def spread(ref, base):
        part = lambda at, h: ref.at[pl.ds(base + at * NZ + 2 * h, 2), pl.ds(c * HALF, HALF)]
        line = lambda at: ref.at[pl.ds(base + at * NZ, NZ), pl.ds(c * HALF, HALF)]
        ring = RingGather(w, part, x, to_x)
        ring.start()
        across = [w.go(line(x), line(x), core)]
        ring.forward()
        ring.finish_near()
        for at in (ring.left, ring.right):
            across.append(w.go(line(at), line(at), core))
        ring.finish_far()
        far = (x + 2) % NX
        across.append(w.go(line(far), line(far), core))
        return across

    ext_core = spread(ext, 0)
    for copy in z_f:
        copy.wait_recv()
    own[0] = total(sum_f[z], from_z_f[0], from_z_f[1], from_z_f[2])

    g_send, g_recv, g_core = w.take(SLOTS), w.take(NM), w.take(NM)
    g_copies = [
        w.make(own.at[s], grad.at[my_rows], {"mp": 2 * s + c}, g_send + s, g_recv + j) for s in range(SLOTS)
    ]
    primary = c == zl

    def send_g(s):
        @pl.when(j != 2 * s + c)
        def _():
            g_copies[s].start()

        @pl.when(j == 2 * s + c)
        def _():
            grad[my_rows] = own[s]

    send_g(0)
    for copy in ext_core:
        copy.wait_recv()
    for s in range(1, SLOTS):
        own[s] = ext[extra_of[s]]
        send_g(s)

    loads[3].wait()
    loads[4].wait()
    n_send, n_recv = w.take(SLOTS), w.take(NM)
    n_copies = []
    for s in range(SLOTS):
        held = jnp.full((ROWS, COLS), occupied[s]) > 0
        g = own[s].astype(F32)
        m = 0.9 * fv[s] + 0.1 * g
        v = 0.95 * sv[s] + 0.05 * g * g
        first_out[s] = jnp.where(held, m, fv[s])
        second_out[s] = jnp.where(held, v, sv[s])
        a = m / (jnp.sqrt(v) + 1e-8)
        length = jnp.broadcast_to(jnp.sqrt(jnp.sum(a * a, axis=1, keepdims=True)), (ROWS, 128))
        length = jnp.sum(jnp.where(lanes == lines, length, 0.0), axis=0, keepdims=True)
        norms[s] = jnp.broadcast_to(length, (8, 128))
        copy = w.make(norms.at[s], norms_in.at[j], device_of(x, z, 1, 2 * s + c), n_send + s, n_recv + j)
        here = (c == 1) & (j == 2 * s + c)
        n_copies.append((here, copy))

        @pl.when(jnp.logical_not(here))
        def _():
            copy.start()

        @pl.when(here)
        def _():
            norms_in[j] = norms[s]

    handed = [
        w.make(grad.at[pl.ds(i * ROWS, ROWS)], grad.at[pl.ds(i * ROWS, ROWS)], core, g_core + i, g_core + i)
        for i in range(NM)
    ]

    @pl.when(primary)
    def _():
        for i in range(NM):

            @pl.when(j != i)
            def _():
                w.make(own.at[0], grad.at[pl.ds(i * ROWS, ROWS)], core, g_send, g_recv + i).wait_recv()

            handed[i].start()

    @pl.when(jnp.logical_not(primary))
    def _():
        for i in range(NM):
            handed[i].wait_recv()

    @pl.when(c == 0)
    def _():
        g = grad[...]
        mat[...] = lax.dot_general(g, g, (((1,), (1,)), ((), ())), preferred_element_type=F32)

    @pl.when(c == 1)
    def _():
        g = grad[...]
        mat[...] = lax.dot_general(g, g, (((0,), (0,)), ((), ())), preferred_element_type=F32)

    for i in range(NM):

        @pl.when(jnp.logical_not((zl == c) & (j == i)))
        def _():
            w.make(lv.at[0], stat.at[pl.ds(i * ROWS, ROWS)], core, stat_send, stat_recv + i).wait_recv()

    term[...] = mat[...].astype(BF16)
    t_send, t_recv = w.take(NM), w.take(2 * SLOTS)
    t_copies = []
    for i in range(NM):
        copy = w.make(
            term.at[pl.ds(i * ROWS, ROWS)], terms.at[c, y], device_of(x, z, zl, i), t_send + i,
            t_recv + c * SLOTS + y,
        )
        here = (zl == c) & (j == i)
        t_copies.append((here, copy))

        @pl.when(jnp.logical_not(here))
        def _():
            copy.start()

        @pl.when(here)
        def _():
            terms[c, y] = term[pl.ds(i * ROWS, ROWS)]

    whole = 0.9 * stat[...] + 0.1 * mat[...]
    mat[...] = whole
    frobenius = jnp.sqrt(jnp.sum(whole * whole, keepdims=True))
    scaling = 5.0 / (2.0 * frobenius)
    start = jnp.sqrt(jnp.sqrt(scaling)).astype(BF16).astype(F32)
    diagonal = lax.broadcasted_iota(jnp.int32, (ORDER, ORDER), 0) == lax.broadcasted_iota(
        jnp.int32, (ORDER, ORDER), 1
    )
    five = jnp.where(diagonal, 5.0, 0.0).astype(F32)
    current[...] = (scaling * mat[...]).astype(BF16)
    factor[...] = ((five - current[...].astype(F32)) * 0.25).astype(BF16)
    root[...] = (start * factor[...].astype(F32)).astype(BF16)

    def sweep(_, carry):
        power[...] = mm(factor[...], factor[...]).astype(BF16)
        power[...] = mm(power[...], power[...]).astype(BF16)
        current[...] = mm(power[...], current[...]).astype(BF16)
        factor[...] = ((five - current[...].astype(F32)) * 0.25).astype(BF16)
        root[...] = mm(root[...], factor[...]).astype(BF16)
        return carry

    lax.fori_loop(0, ITERS - 1, sweep, 0)

    step = 2 * ROWS
    count = ORDER // step
    h_at = w.take(count)
    h_copies = [
        w.make(half.at[pl.ds(i * step, step)], half_in.at[pl.ds(i * step, step)], core, h_at + i, h_at + i)
        for i in range(count)
    ]
    d_send, d_recv = w.take(NM), w.take(SLOTS)
    d_copies = [
        w.make(
            turned.at[pl.ds(i * ROWS, ROWS)], update.at[y], device_of(x, z, zl, i), d_send + i, d_recv + y
        )
        for i in range(NM)
    ]

    @pl.when(c == 0)
    def _():
        for i in range(count):
            rows = pl.ds(i * step, step)
            half[rows] = mm(root[rows], grad[...]).astype(BF16)
            h_copies[i].start()

    @pl.when(c == 1)
    def _():
        for i in range(NM):

            @pl.when(jnp.logical_not((zl == 1) & (j == i)))
            def _():
                w.make(norms.at[0], norms_in.at[i], core, n_send, n_recv + i).wait_recv()

        for i in range(count):
            rows = pl.ds(i * step, step)
            h_copies[i].wait_recv()
            s = mm(half_in[rows], root[...])
            for u in range(2):
                to = 2 * i + u
                here = (zl == 1) & (j == to)
                piece = s[u * ROWS : (u + 1) * ROWS]
                length = jnp.sqrt(jnp.sum(piece * piece, axis=1, keepdims=True)) + 1e-6
                adam = jnp.broadcast_to(norms_in[to, 0:1], (ROWS, 128))
                adam = jnp.sum(jnp.where(lanes == lines, adam, 0.0), axis=1, keepdims=True)
                turned[pl.ds(to * ROWS, ROWS)] = (piece * (adam / length)).astype(BF16)

                @pl.when(jnp.logical_not(here))
                def _():
                    d_copies[to].start()

                @pl.when(here)
                def _():
                    update[y] = turned[pl.ds(to * ROWS, ROWS)]

    def wait_update(s):
        @pl.when(jnp.logical_not((c == 1) & (j == 2 * s + c)))
        def _():
            w.make(turned.at[pl.ds(0, ROWS)], update.at[s], core, d_send, d_recv + s).wait_recv()

    here_f = c * NK + x * NZ + z
    wait_update(0)
    all_of[here_f] = update[0]
    f_z = [w.go(all_of.at[here_f], all_of.at[here_f], dp_of(x, (z + k) % NZ, c)) for k in FAR_FIRST]

    def ring_of(k):
        at_z = (z + NZ - k) % NZ
        part = lambda at, h: all_of.at[c * NK + at * NZ + at_z, pl.ds(h * HALF, HALF)]
        return RingGather(w, part, x, to_x)

    rings = {k: ring_of(k) for k in range(NZ)}
    rings[0].start()
    for s in range(1, SLOTS):
        wait_update(s)

    def picked(e, which):
        at = mine_of[e]
        value = update[at, pl.ds(which * HALF, HALF)]
        return jnp.where(jnp.full(value.shape, at) > 0, value.astype(F32), 0.0)

    for e in range(EXTRAS):
        send_d[e] = picked(e, other).astype(BF16)
    core_d = w.go(send_d, recv_d, core)
    core_d.wait_recv()
    ring_d = RingReduce(w, acc_d, pass_d, came_d, x, to_x)
    for k in turns:
        for q in range(NZ):
            e = ((x + k) % NX) * NZ + q
            acc_d[e] = (picked(e, c) + recv_d[e].astype(F32)).astype(BF16)
        if k == 2:
            ring_d.send_far()
        if k == 1:
            ring_d.send_right()
        if k == 3:
            ring_d.send_left()
    for copy, k in sorted(zip(f_z, FAR_FIRST), key=lambda pair: pair[1] == 2):
        copy.wait_recv()
        rings[k].start()
    f_line = lambda at: all_of.at[pl.ds(c * NK + at * NZ, NZ)]
    f_core = [w.go(f_line(x), f_line(x), core)]
    ring_d.forward()
    rings[0].forward()
    ring_d.finish(sum_d)
    z_d = [w.go(sum_d.at[(z + k) % NZ], from_z_d.at[k - 1], dp_of(x, (z + k) % NZ, c)) for k in FAR_FIRST]
    for k in (1, 3, 2):
        rings[k].forward()
    for copy in z_d:
        copy.wait_recv()
    here_e = (OWNERS + x * NZ + z, pl.ds(c * HALF, HALF))
    all_of[here_e] = total(sum_d[z], from_z_d[0], from_z_d[1], from_z_d[2])
    mine = all_of.at[here_e]
    z_g = [w.go(mine, mine, dp_of(x, (z + k) % NZ, c)) for k in FAR_FIRST]

    for role in range(2):
        for s in range(SLOTS):

            @pl.when(jnp.logical_not((role == c) & (j == 2 * s + c)))
            def _():
                w.make(
                    term.at[pl.ds(0, ROWS)], terms.at[role, s], core, t_send, t_recv + role * SLOTS + s
                ).wait_recv()

            old, new = ((lv, left_out), (rv, right_out))[role]
            held = jnp.full((ROWS, COLS), occupied[s]) > 0
            new[s] = jnp.where(held, 0.9 * old[s] + 0.1 * terms[role, s].astype(F32), old[s])

    for copy in z_g:
        copy.wait_recv()
    e_core = spread(all_of, OWNERS)
    for k in range(NZ):
        rings[k].finish_near()
    for at in ((x + 3) % NX, (x + 1) % NX):
        f_core.append(w.go(f_line(at), f_line(at), core))
    for k in range(NZ):
        rings[k].finish_far()
    f_core.append(w.go(f_line((x + 2) % NX), f_line((x + 2) % NX), core))
    for copy in f_core + e_core:
        copy.wait_recv()
    for b in range(BLOCKS):
        out[b] = all_of[place_of[b]]

    for copy in w.sent:
        copy.wait_send()
    for here, copy in stat_copies + n_copies + t_copies:

        @pl.when(jnp.logical_not(here))
        def _():
            copy.wait_send()

    for s in range(SLOTS):

        @pl.when(j != 2 * s + c)
        def _():
            g_copies[s].wait_send()

    @pl.when(primary)
    def _():
        for copy in handed:
            copy.wait_send()

    @pl.when(c == 0)
    def _():
        for copy in h_copies:
            copy.wait_send()

    @pl.when(c == 1)
    def _():
        for i in range(NM):

            @pl.when(jnp.logical_not((zl == 1) & (j == i)))
            def _():
                d_copies[i].wait_send()


def whole_step(order, place_of, occupied, extra_of, mine_of, grads, left, right, first, second):
    state = jax.ShapeDtypeStruct((SLOTS, ROWS, COLS), F32)
    v = lambda *shape, kind=BF16: pltpu.VMEM(shape, kind)
    dma = pltpu.SemaphoreType.DMA
    half = (HALF, COLS)
    full = (ROWS, COLS)
    return pl.pallas_call(
        kernel,
        out_shape=(jax.ShapeDtypeStruct((BLOCKS, ROWS, COLS), BF16), state, state, state, state),
        in_specs=[SMEM] * 5 + [ANY] * 5,
        out_specs=(VMEM,) * 5,
        scratch_shapes=[v(BLOCKS, *full)]
        + [v(SLOTS, *full, kind=F32)] * 4
        + [
            v(NK, *full), v(NK, *half), v(NK, *full), v(NK, *half), v(NK, *full), v(NK, *half),
            v(2, 2, *full), v(2, 2, *half), v(2, NZ, *full), v(2, NZ, *half), v(NZ, *full), v(NZ, *half),
            v(3, *full), v(3, *half), v(EXTRAS, *full), v(SLOTS, *full),
        ]
        + [
            v(ORDER, COLS), v(ORDER, COLS, kind=F32), v(SLOTS, 8, 128, kind=F32), v(NM, 8, 128, kind=F32),
            v(ORDER, COLS, kind=F32), v(ORDER, COLS), v(2, SLOTS, *full),
        ]
        + [v(ORDER, COLS)] * 7
        + [v(SLOTS, *full)]
        + [
            v(BLOCKS, *full), v(EXTRAS, *half), v(EXTRAS, *half), v(EXTRAS, *half), v(2, 2, *half),
            v(2, NZ, *half), v(NZ, *half), v(3, *half),
        ]
        + [dma((SEMS,)), dma((SEMS,)), dma((5,)), dma((1,))],
        compiler_params=pltpu.CompilerParams(
            collective_id=0, has_side_effects=True, vmem_limit_bytes=56 << 20
        ),
        name="shampoo_step",
    )(order, place_of, occupied, extra_of, mine_of, grads, left, right, first, second)


def tables(owners):
    owner = owners[:, 0]
    me = lax.axis_index("dp")
    spots = jnp.arange(BLOCKS, dtype=jnp.int32)
    earlier = spots[None, :] < spots[:, None]
    slot = jnp.sum((owner[:, None] == owner[None, :]) & earlier, axis=1, dtype=jnp.int32)
    again = slot > 0
    rank = jnp.sum(again[None, :] & earlier, axis=1, dtype=jnp.int32)
    sorted_at = jnp.where(again, OWNERS + rank, owner)
    order = jnp.sum(jnp.where(sorted_at[None, :] == spots[:, None], spots[None, :], 0), axis=1)
    place_of = jnp.where(again, OWNERS + rank, (owner % NC) * NK + owner // NC)
    mine = owner == me
    slots = jnp.arange(SLOTS, dtype=jnp.int32)
    holds = mine[None, :] & (slot[None, :] == slots[:, None])
    occupied = jnp.sum(holds, axis=1, dtype=jnp.int32)
    extra_of = jnp.sum(jnp.where(holds & again[None, :], rank[None, :], 0), axis=1)
    extras = jnp.arange(EXTRAS, dtype=jnp.int32)
    held = (mine & again)[None, :] & (rank[None, :] == extras[:, None])
    mine_of = jnp.sum(jnp.where(held, slot[None, :], 0), axis=1)
    return order, place_of, occupied, extra_of, mine_of


def body(grads, owners, left_stat, right_stat, first_moment, second_moment):
    direction, *states = whole_step(
        *tables(owners), grads[0], left_stat[0], right_stat[0], first_moment[0], second_moment[0]
    )
    return (direction, *(state[None] for state in states))


def solution(mesh):
    split = P("dp", None, "mp", None)
    return jax.shard_map(
        body,
        mesh=mesh,
        in_specs=(split, P(), split, split, split, split),
        out_specs=(P(None, "mp", None), split, split, split, split),
        check_vma=False,
    )
```

```python
import jax
import jax.numpy as jnp
from jax import lax
from jax.experimental import pallas as pl
from jax.experimental.pallas import tpu as pltpu
from jax.sharding import PartitionSpec as P

ITERS = 6
MESH = pl.DeviceIdType.MESH
VMEM = pl.BlockSpec(memory_space=pltpu.VMEM)
SMEM = pl.BlockSpec(memory_space=pltpu.SMEM)
ANY = pl.BlockSpec(memory_space=pl.ANY)
F32, BF16 = jnp.float32, jnp.bfloat16
NX, NZ, NC, NM = 4, 4, 2, 8
NK = NX * NZ
ROWS, COLS, HALF = 64, 512, 32
ORDER = NM * ROWS
SLOTS = 4
BLOCKS = 48
OWNERS = NK * NC
EXTRAS = BLOCKS - OWNERS
FAR_FIRST = (2, 1, 3)
SEMS = 192
PLACE_OF, OCCUPIED, EXTRA_OF, MINE_OF, TABLE = 48, 96, 100, 104, 128


def dp_of(x, z, c):
    return {"dp": (x * NZ + z) * NC + c}


def device_of(x, z, c, j):
    return {"dp": (x * NZ + z) * NC + c, "mp": j}


def total(*parts):
    value = parts[0].astype(F32)
    for part in parts[1:]:
        value = value + part.astype(F32)
    return value.astype(BF16)


def mm(a, b):
    return jnp.dot(a, b, preferred_element_type=F32)


class Wires:
    def __init__(self, send, recv):
        self.send, self.recv, self.used, self.sent = send, recv, 0, []

    def take(self, count):
        self.used += count
        assert self.used <= SEMS
        return self.used - count

    def make(self, src, dst, device, at_send, at_recv):
        return pltpu.make_async_remote_copy(
            src_ref=src, dst_ref=dst, send_sem=self.send.at[at_send], recv_sem=self.recv.at[at_recv],
            device_id=device, device_id_type=MESH,
        )

    def go(self, src, dst, device):
        at = self.take(1)
        copy = self.make(src, dst, device, at, at)
        copy.start()
        self.sent.append(copy)
        return copy


class RingReduce:
    def __init__(self, wires, acc, passed, came, x, to):
        self.wires, self.acc, self.passed, self.came, self.x, self.to = wires, acc, passed, came, x, to
        self.right, self.left, self.far = (x + 1) % NX, (x + 3) % NX, (x + 2) % NX

    def part(self, at, h):
        return self.acc.at[pl.ds(at * NZ + 2 * h, 2)]

    def send_far(self):
        self.a = self.wires.go(self.part(self.far, 0), self.passed.at[0], self.to(self.right))
        self.b = self.wires.go(self.part(self.far, 1), self.passed.at[1], self.to(self.left))

    def send_right(self):
        self.c = self.wires.go(self.part(self.right, 1), self.came.at[0, pl.ds(2, 2)], self.to(self.right))

    def send_left(self):
        self.d = self.wires.go(self.part(self.left, 0), self.came.at[1, pl.ds(0, 2)], self.to(self.left))

    def forward(self):
        self.a.wait_recv()
        for q in range(2):
            at = self.right * NZ + q
            self.acc[at] = total(self.acc[at], self.passed[0, q])
        self.e = self.wires.go(self.part(self.right, 0), self.came.at[0, pl.ds(0, 2)], self.to(self.right))
        self.b.wait_recv()
        for q in range(2):
            at = self.left * NZ + 2 + q
            self.acc[at] = total(self.acc[at], self.passed[1, q])
        self.f = self.wires.go(self.part(self.left, 1), self.came.at[1, pl.ds(2, 2)], self.to(self.left))

    def finish(self, out):
        for copy in (self.c, self.d, self.e, self.f):
            copy.wait_recv()
        for q in range(NZ):
            out[q] = total(self.acc[self.x * NZ + q], self.came[0, q], self.came[1, q])


class RingGather:
    def __init__(self, wires, part, x, to):
        self.wires, self.part = wires, part
        self.x, self.right, self.left = x, (x + 1) % NX, (x + 3) % NX
        self.to_right, self.to_left = to(self.right), to(self.left)

    def push(self, at, h, device):
        return self.wires.go(self.part(at, h), self.part(at, h), device)

    def start(self):
        self.a = self.push(self.x, 0, self.to_right)
        self.b = self.push(self.x, 1, self.to_left)
        self.c = self.push(self.x, 1, self.to_right)
        self.d = self.push(self.x, 0, self.to_left)

    def forward(self):
        self.a.wait_recv()
        self.e = self.push(self.left, 0, self.to_right)
        self.b.wait_recv()
        self.f = self.push(self.right, 1, self.to_left)

    def finish_near(self):
        self.c.wait_recv()
        self.d.wait_recv()

    def finish_far(self):
        self.e.wait_recv()
        self.f.wait_recv()


def kernel(
    table, grads, left, right, first, second,
    all_out, left_hbm, right_hbm, first_hbm, second_hbm,
    gv, lv, rv, fv, sv, all_of, left_out, right_out, first_out, second_out,
    send_f, send_e, recv_f, recv_e, acc_f, acc_e, pass_f, pass_e, came_f, came_e, sum_f, sum_e,
    from_z_f, from_z_e, ext, own,
    grad, stat, norms, norms_in, mat, term, terms, power, factor, current, root, half, half_in, turned, update,
    send_d, recv_d, acc_d, pass_d, came_d, sum_d, from_z_d,
    send_sem, recv_sem, load_sem, store_sem,
):
    me = lax.axis_index("dp")
    j = lax.axis_index("mp")
    x, z, c = me // (NZ * NC), (me // NC) % NZ, me % NC
    y, zl = j // 2, j % 2
    other = 1 - c
    core = dp_of(x, z, other)
    to_x = lambda at: dp_of(at, z, c)
    w = Wires(send_sem, recv_sem)
    my_rows = pl.ds(j * ROWS, ROWS)
    lanes = lax.broadcasted_iota(jnp.int32, (ROWS, 128), 1)
    lines = lax.broadcasted_iota(jnp.int32, (ROWS, 128), 0)

    loads = [
        pltpu.make_async_copy(src, dst, load_sem.at[i])
        for i, (src, dst) in enumerate(((grads, gv), (left, lv), (right, rv), (first, fv), (second, sv)))
    ]
    for copy in loads:
        copy.start()

    barrier = pltpu.get_barrier_semaphore()
    greeted = 0
    for k in range(1, 4):
        for device in (dp_of((x + k) % NX, z, c), dp_of(x, (z + k) % NZ, c)):
            pl.semaphore_signal(barrier, inc=1, device_id=device, device_id_type=MESH)
            greeted += 1
    for k in range(NM):
        for which in range(NC):
            if k or which:
                device = device_of(x, z, (c + which) % NC, (j + k) % NM)
                pl.semaphore_signal(barrier, inc=1, device_id=device, device_id_type=MESH)
                greeted += 1
    pl.semaphore_wait(barrier, greeted)

    loads[0].wait()
    for k in range(NK):
        send_e[k] = gv[table[OWNERS + k], pl.ds(other * HALF, HALF)]
    core_e = w.go(send_e, recv_e, core)
    turns = (2, 1, 3, 0)
    core_f = []
    for k in turns:
        at = (x + k) % NX
        for q in range(NZ):
            send_f[at * NZ + q] = gv[table[(at * NZ + q) * NC + other]]
        rows = pl.ds(at * NZ, NZ)
        core_f.append(w.go(send_f.at[rows], recv_f.at[rows], core))

    ring_e = RingReduce(w, acc_e, pass_e, came_e, x, to_x)
    ring_f = RingReduce(w, acc_f, pass_f, came_f, x, to_x)
    core_e.wait_recv()

    def add_e(step):
        for q in range(NZ):
            k = ((x + turns[step]) % NX) * NZ + q
            acc_e[k] = total(gv[table[OWNERS + k], pl.ds(c * HALF, HALF)], recv_e[k])

    add_e(0)
    ring_e.send_far()
    add_e(1)
    ring_e.send_right()
    add_e(2)
    ring_e.send_left()
    add_e(3)

    loads[1].wait()
    loads[2].wait()
    stat_send, stat_recv = w.take(2 * SLOTS), w.take(NM)
    stat_copies = []
    for s in range(SLOTS):
        for role, source in enumerate((lv, rv)):
            copy = w.make(
                source.at[s], stat.at[my_rows], device_of(x, z, role, 2 * s + c), stat_send + 2 * s + role,
                stat_recv + j,
            )
            here = (c == role) & (j == 2 * s + c)
            stat_copies.append((here, copy))

            @pl.when(jnp.logical_not(here))
            def _():
                copy.start()

            @pl.when(here)
            def _():
                stat[my_rows] = source[s]

    def add_f(step):
        at = (x + turns[step]) % NX
        core_f[step].wait_recv()
        for q in range(NZ):
            acc_f[at * NZ + q] = total(gv[table[(at * NZ + q) * NC + c]], recv_f[at * NZ + q])

    add_f(0)
    ring_e.forward()
    ring_f.send_far()
    add_f(1)
    ring_f.send_right()
    add_f(2)
    ring_f.send_left()
    add_f(3)
    ring_e.finish(sum_e)
    z_e = [w.go(sum_e.at[(z + k) % NZ], from_z_e.at[k - 1], dp_of(x, (z + k) % NZ, c)) for k in FAR_FIRST]
    ring_f.forward()
    for copy in z_e:
        copy.wait_recv()
    mine = ext.at[x * NZ + z, pl.ds(c * HALF, HALF)]
    ext[x * NZ + z, pl.ds(c * HALF, HALF)] = total(sum_e[z], from_z_e[0], from_z_e[1], from_z_e[2])
    z_g = [w.go(mine, mine, dp_of(x, (z + k) % NZ, c)) for k in FAR_FIRST]
    ring_f.finish(sum_f)
    z_f = [w.go(sum_f.at[(z + k) % NZ], from_z_f.at[k - 1], dp_of(x, (z + k) % NZ, c)) for k in FAR_FIRST]
    for copy in z_g:
        copy.wait_recv()

    def spread(ref, base):
        part = lambda at, h: ref.at[pl.ds(base + at * NZ + 2 * h, 2), pl.ds(c * HALF, HALF)]
        line = lambda at: ref.at[pl.ds(base + at * NZ, NZ), pl.ds(c * HALF, HALF)]
        ring = RingGather(w, part, x, to_x)
        ring.start()
        across = [w.go(line(x), line(x), core)]
        ring.forward()
        ring.finish_near()
        for at in (ring.left, ring.right):
            across.append(w.go(line(at), line(at), core))
        ring.finish_far()
        far = (x + 2) % NX
        across.append(w.go(line(far), line(far), core))
        return across

    ext_core = spread(ext, 0)
    for copy in z_f:
        copy.wait_recv()
    own[0] = total(sum_f[z], from_z_f[0], from_z_f[1], from_z_f[2])

    g_send, g_recv, g_core = w.take(SLOTS), w.take(NM), w.take(NM)
    g_copies = [
        w.make(own.at[s], grad.at[my_rows], {"mp": 2 * s + c}, g_send + s, g_recv + j) for s in range(SLOTS)
    ]
    primary = c == zl

    def send_g(s):
        @pl.when(j != 2 * s + c)
        def _():
            g_copies[s].start()

        @pl.when(j == 2 * s + c)
        def _():
            grad[my_rows] = own[s]

    send_g(0)
    for copy in ext_core:
        copy.wait_recv()
    for s in range(1, SLOTS):
        own[s] = ext[table[EXTRA_OF + s]]
        send_g(s)

    stores = []

    def store(src, dst):
        copy = pltpu.make_async_copy(src, dst, store_sem.at[len(stores)])
        copy.start()
        stores.append(copy)

    loads[3].wait()
    loads[4].wait()
    n_send, n_recv = w.take(SLOTS), w.take(NM)
    n_copies = []
    for s in range(SLOTS):
        held = jnp.full((ROWS, COLS), table[OCCUPIED + s]) > 0
        g = own[s].astype(F32)
        m = 0.9 * fv[s] + 0.1 * g
        v = 0.95 * sv[s] + 0.05 * g * g
        first_out[s] = jnp.where(held, m, fv[s])
        second_out[s] = jnp.where(held, v, sv[s])
        a = m / (jnp.sqrt(v) + 1e-8)
        length = jnp.broadcast_to(jnp.sqrt(jnp.sum(a * a, axis=1, keepdims=True)), (ROWS, 128))
        length = jnp.sum(jnp.where(lanes == lines, length, 0.0), axis=0, keepdims=True)
        norms[s] = jnp.broadcast_to(length, (8, 128))
        copy = w.make(norms.at[s], norms_in.at[j], device_of(x, z, 1, 2 * s + c), n_send + s, n_recv + j)
        here = (c == 1) & (j == 2 * s + c)
        n_copies.append((here, copy))

        @pl.when(jnp.logical_not(here))
        def _():
            copy.start()

        @pl.when(here)
        def _():
            norms_in[j] = norms[s]

    store(first_out, first_hbm)
    store(second_out, second_hbm)
    handed = [
        w.make(grad.at[pl.ds(i * ROWS, ROWS)], grad.at[pl.ds(i * ROWS, ROWS)], core, g_core + i, g_core + i)
        for i in range(NM)
    ]

    @pl.when(primary)
    def _():
        for i in range(NM):

            @pl.when(j != i)
            def _():
                w.make(own.at[0], grad.at[pl.ds(i * ROWS, ROWS)], core, g_send, g_recv + i).wait_recv()

            handed[i].start()

    @pl.when(jnp.logical_not(primary))
    def _():
        for i in range(NM):
            handed[i].wait_recv()

    @pl.when(c == 0)
    def _():
        g = grad[...]
        mat[...] = lax.dot_general(g, g, (((1,), (1,)), ((), ())), preferred_element_type=F32)

    @pl.when(c == 1)
    def _():
        g = grad[...]
        mat[...] = lax.dot_general(g, g, (((0,), (0,)), ((), ())), preferred_element_type=F32)

    for i in range(NM):

        @pl.when(jnp.logical_not((zl == c) & (j == i)))
        def _():
            w.make(lv.at[0], stat.at[pl.ds(i * ROWS, ROWS)], core, stat_send, stat_recv + i).wait_recv()

    term[...] = mat[...].astype(BF16)
    t_send, t_recv = w.take(NM), w.take(2 * SLOTS)
    t_copies = []
    for i in range(NM):
        copy = w.make(
            term.at[pl.ds(i * ROWS, ROWS)], terms.at[c, y], device_of(x, z, zl, i), t_send + i,
            t_recv + c * SLOTS + y,
        )
        here = (zl == c) & (j == i)
        t_copies.append((here, copy))

        @pl.when(jnp.logical_not(here))
        def _():
            copy.start()

        @pl.when(here)
        def _():
            terms[c, y] = term[pl.ds(i * ROWS, ROWS)]

    whole = 0.9 * stat[...] + 0.1 * mat[...]
    mat[...] = whole
    frobenius = jnp.sqrt(jnp.sum(whole * whole, keepdims=True))
    scaling = 5.0 / (2.0 * frobenius)
    start = jnp.sqrt(jnp.sqrt(scaling)).astype(BF16).astype(F32)
    diagonal = lax.broadcasted_iota(jnp.int32, (ORDER, ORDER), 0) == lax.broadcasted_iota(
        jnp.int32, (ORDER, ORDER), 1
    )
    five = jnp.where(diagonal, 5.0, 0.0).astype(F32)
    current[...] = (scaling * mat[...]).astype(BF16)
    factor[...] = ((five - current[...].astype(F32)) * 0.25).astype(BF16)
    root[...] = (start * factor[...].astype(F32)).astype(BF16)

    def sweep(_, carry):
        power[...] = mm(factor[...], factor[...]).astype(BF16)
        power[...] = mm(power[...], power[...]).astype(BF16)
        current[...] = mm(power[...], current[...]).astype(BF16)
        factor[...] = ((five - current[...].astype(F32)) * 0.25).astype(BF16)
        root[...] = mm(root[...], factor[...]).astype(BF16)
        return carry

    lax.fori_loop(0, ITERS - 1, sweep, 0)

    step = 2 * ROWS
    count = ORDER // step
    h_at = w.take(count)
    h_copies = [
        w.make(half.at[pl.ds(i * step, step)], half_in.at[pl.ds(i * step, step)], core, h_at + i, h_at + i)
        for i in range(count)
    ]
    d_send, d_recv = w.take(NM), w.take(SLOTS)
    d_copies = [
        w.make(
            turned.at[pl.ds(i * ROWS, ROWS)], update.at[y], device_of(x, z, zl, i), d_send + i, d_recv + y
        )
        for i in range(NM)
    ]

    @pl.when(c == 0)
    def _():
        for i in range(count):
            rows = pl.ds(i * step, step)
            half[rows] = mm(root[rows], grad[...]).astype(BF16)
            h_copies[i].start()

    @pl.when(c == 1)
    def _():
        for i in range(NM):

            @pl.when(jnp.logical_not((zl == 1) & (j == i)))
            def _():
                w.make(norms.at[0], norms_in.at[i], core, n_send, n_recv + i).wait_recv()

        for i in range(count):
            rows = pl.ds(i * step, step)
            h_copies[i].wait_recv()
            s = mm(half_in[rows], root[...])
            for u in range(2):
                to = 2 * i + u
                here = (zl == 1) & (j == to)
                piece = s[u * ROWS : (u + 1) * ROWS]
                length = jnp.sqrt(jnp.sum(piece * piece, axis=1, keepdims=True)) + 1e-6
                adam = jnp.broadcast_to(norms_in[to, 0:1], (ROWS, 128))
                adam = jnp.sum(jnp.where(lanes == lines, adam, 0.0), axis=1, keepdims=True)
                turned[pl.ds(to * ROWS, ROWS)] = (piece * (adam / length)).astype(BF16)

                @pl.when(jnp.logical_not(here))
                def _():
                    d_copies[to].start()

                @pl.when(here)
                def _():
                    update[y] = turned[pl.ds(to * ROWS, ROWS)]

    def wait_update(s):
        @pl.when(jnp.logical_not((c == 1) & (j == 2 * s + c)))
        def _():
            w.make(turned.at[pl.ds(0, ROWS)], update.at[s], core, d_send, d_recv + s).wait_recv()

    here_f = c * NK + x * NZ + z
    wait_update(0)
    all_of[here_f] = update[0]
    f_z = [w.go(all_of.at[here_f], all_of.at[here_f], dp_of(x, (z + k) % NZ, c)) for k in FAR_FIRST]

    def ring_of(k):
        at_z = (z + NZ - k) % NZ
        part = lambda at, h: all_of.at[c * NK + at * NZ + at_z, pl.ds(h * HALF, HALF)]
        return RingGather(w, part, x, to_x)

    rings = {k: ring_of(k) for k in range(NZ)}
    for q in range(1, SLOTS):
        wait_update(q)

    def picked(e, which):
        at = table[MINE_OF + e]
        value = update[at, pl.ds(which * HALF, HALF)]
        return jnp.where(jnp.full(value.shape, at) > 0, value.astype(F32), 0.0)

    for e in range(EXTRAS):
        send_d[e] = picked(e, other).astype(BF16)
    core_d = w.go(send_d, recv_d, core)
    ring_d = RingReduce(w, acc_d, pass_d, came_d, x, to_x)
    core_d.wait_recv()
    for k, send in ((2, ring_d.send_far), (1, ring_d.send_right), (3, ring_d.send_left), (0, None)):
        for q in range(NZ):
            e = ((x + k) % NX) * NZ + q
            acc_d[e] = (picked(e, c) + recv_d[e].astype(F32)).astype(BF16)
        if send:
            send()
    ring_d.forward()
    rings[0].start()
    ring_d.finish(sum_d)
    z_d = [w.go(sum_d.at[(z + k) % NZ], from_z_d.at[k - 1], dp_of(x, (z + k) % NZ, c)) for k in FAR_FIRST]
    for copy, k in sorted(zip(f_z, FAR_FIRST), key=lambda pair: pair[1] == 2):
        copy.wait_recv()
        rings[k].start()
    f_line = lambda at: all_of.at[pl.ds(c * NK + at * NZ, NZ)]
    f_core = [w.go(f_line(x), f_line(x), core)]
    rings[0].forward()
    for copy in z_d:
        copy.wait_recv()
    here_e = (OWNERS + x * NZ + z, pl.ds(c * HALF, HALF))
    all_of[here_e] = total(sum_d[z], from_z_d[0], from_z_d[1], from_z_d[2])
    mine = all_of.at[here_e]
    z_g = [w.go(mine, mine, dp_of(x, (z + k) % NZ, c)) for k in FAR_FIRST]
    for k in (1, 3, 2):
        rings[k].forward()

    for role in range(2):
        for s in range(SLOTS):

            @pl.when(jnp.logical_not((role == c) & (j == 2 * s + c)))
            def _():
                w.make(
                    term.at[pl.ds(0, ROWS)], terms.at[role, s], core, t_send, t_recv + role * SLOTS + s
                ).wait_recv()

            old, new = ((lv, left_out), (rv, right_out))[role]
            held = jnp.full((ROWS, COLS), table[OCCUPIED + s]) > 0
            new[s] = jnp.where(held, 0.9 * old[s] + 0.1 * terms[role, s].astype(F32), old[s])

    store(left_out, left_hbm)
    store(right_out, right_hbm)
    for copy in z_g:
        copy.wait_recv()
    e_core = spread(all_of, OWNERS)
    for k in range(NZ):
        rings[k].finish_near()
    for at in ((x + 3) % NX, (x + 1) % NX):
        f_core.append(w.go(f_line(at), f_line(at), core))
    for k in range(NZ):
        rings[k].finish_far()
    f_core.append(w.go(f_line((x + 2) % NX), f_line((x + 2) % NX), core))
    for copy in f_core:
        copy.wait_recv()
    firsts = pl.ds(0, OWNERS)
    store(all_of.at[firsts], all_out.at[firsts])
    for copy in e_core:
        copy.wait_recv()
    extras = pl.ds(OWNERS, EXTRAS)
    store(all_of.at[extras], all_out.at[extras])

    for copy in stores:
        copy.wait()
    for copy in w.sent:
        copy.wait_send()
    for here, copy in stat_copies + n_copies + t_copies:

        @pl.when(jnp.logical_not(here))
        def _():
            copy.wait_send()

    for s in range(SLOTS):

        @pl.when(j != 2 * s + c)
        def _():
            g_copies[s].wait_send()

    @pl.when(primary)
    def _():
        for copy in handed:
            copy.wait_send()

    @pl.when(c == 0)
    def _():
        for copy in h_copies:
            copy.wait_send()

    @pl.when(c == 1)
    def _():
        for i in range(NM):

            @pl.when(jnp.logical_not((zl == 1) & (j == i)))
            def _():
                d_copies[i].wait_send()


def whole_step(table, grads, left, right, first, second):
    state = jax.ShapeDtypeStruct((SLOTS, ROWS, COLS), F32)
    v = lambda *shape, kind=BF16: pltpu.VMEM(shape, kind)
    dma = pltpu.SemaphoreType.DMA
    half = (HALF, COLS)
    full = (ROWS, COLS)
    return pl.pallas_call(
        kernel,
        out_shape=(jax.ShapeDtypeStruct((BLOCKS, ROWS, COLS), BF16), state, state, state, state),
        in_specs=[SMEM] + [ANY] * 5,
        out_specs=(ANY,) * 5,
        scratch_shapes=[v(BLOCKS, *full)]
        + [v(SLOTS, *full, kind=F32)] * 4
        + [v(BLOCKS, *full)]
        + [v(SLOTS, *full, kind=F32)] * 4
        + [
            v(NK, *full), v(NK, *half), v(NK, *full), v(NK, *half), v(NK, *full), v(NK, *half),
            v(2, 2, *full), v(2, 2, *half), v(2, NZ, *full), v(2, NZ, *half), v(NZ, *full), v(NZ, *half),
            v(3, *full), v(3, *half), v(EXTRAS, *full), v(SLOTS, *full),
        ]
        + [
            v(ORDER, COLS), v(ORDER, COLS, kind=F32), v(SLOTS, 8, 128, kind=F32), v(NM, 8, 128, kind=F32),
            v(ORDER, COLS, kind=F32), v(ORDER, COLS), v(2, SLOTS, *full),
        ]
        + [v(ORDER, COLS)] * 7
        + [v(SLOTS, *full)]
        + [
            v(EXTRAS, *half), v(EXTRAS, *half), v(EXTRAS, *half), v(2, 2, *half),
            v(2, NZ, *half), v(NZ, *half), v(3, *half),
        ]
        + [dma((SEMS,)), dma((SEMS,)), dma((5,)), dma((7,))],
        compiler_params=pltpu.CompilerParams(
            collective_id=0, has_side_effects=True, vmem_limit_bytes=56 << 20
        ),
        name="shampoo_step",
    )(table, grads, left, right, first, second)


def table_kernel(owner, table, counts):
    me = lax.axis_index("dp")

    def clear(i, carry):
        table[i] = 0
        return carry

    def clear_counts(i, carry):
        counts[i] = 0
        return carry

    lax.fori_loop(OCCUPIED, MINE_OF + EXTRAS, clear, 0)
    lax.fori_loop(0, OWNERS, clear_counts, 0)

    def visit(b, rank):
        o = owner[b]
        slot = counts[o]
        counts[o] = slot + 1
        again = slot > 0
        table[jnp.where(again, OWNERS + rank, o)] = b
        table[PLACE_OF + b] = jnp.where(again, OWNERS + rank, (o % NC) * NK + o // NC)

        @pl.when(o == me)
        def _():
            table[OCCUPIED + slot] = 1

            @pl.when(again)
            def _():
                table[EXTRA_OF + slot] = rank
                table[MINE_OF + rank] = slot

        return rank + again.astype(jnp.int32)

    lax.fori_loop(0, BLOCKS, visit, jnp.int32(0))


def tables(owners):
    return pl.pallas_call(
        table_kernel,
        out_shape=jax.ShapeDtypeStruct((TABLE,), jnp.int32),
        in_specs=[SMEM],
        out_specs=SMEM,
        scratch_shapes=[pltpu.SMEM((OWNERS,), jnp.int32)],
        name="tables",
    )(owners[:, 0])


def output_kernel(table, all_of, a, b, c, d, out, a_out, b_out, c_out, d_out, sems):
    copies = [
        pltpu.make_async_copy(src, dst.at[0], sems.at[BLOCKS + i])
        for i, (src, dst) in enumerate(((a, a_out), (b, b_out), (c, c_out), (d, d_out)))
    ]
    copies += [
        pltpu.make_async_copy(all_of.at[table[PLACE_OF + i]], out.at[i], sems.at[i]) for i in range(BLOCKS)
    ]
    for copy in copies:
        copy.start()
    for copy in copies:
        copy.wait()


def outputs(table, *parts):
    state = jax.ShapeDtypeStruct((1, SLOTS, ROWS, COLS), F32)
    return pl.pallas_call(
        output_kernel,
        out_shape=(jax.ShapeDtypeStruct((BLOCKS, ROWS, COLS), BF16), state, state, state, state),
        in_specs=[SMEM] + [ANY] * 5,
        out_specs=(ANY,) * 5,
        scratch_shapes=[pltpu.SemaphoreType.DMA((BLOCKS + 4,))],
        compiler_params=pltpu.CompilerParams(vmem_limit_bytes=56 << 20),
        name="outputs",
    )(table, *parts)


def body(grads, owners, left_stat, right_stat, first_moment, second_moment):
    table = tables(owners)
    parts = whole_step(table, grads[0], left_stat[0], right_stat[0], first_moment[0], second_moment[0])
    return outputs(table, *parts)


def solution(mesh):
    split = P("dp", None, "mp", None)
    return jax.shard_map(
        body,
        mesh=mesh,
        in_specs=(split, P(), split, split, split, split),
        out_specs=(P(None, "mp", None), split, split, split, split),
        check_vma=False,
    )
```

```python
import jax
import jax.numpy as jnp
from jax import lax
from jax.experimental import pallas as pl
from jax.experimental.pallas import tpu as pltpu
from jax.sharding import PartitionSpec as P

ITERS = 6
MESH = pl.DeviceIdType.MESH
VMEM = pl.BlockSpec(memory_space=pltpu.VMEM)
SMEM = pl.BlockSpec(memory_space=pltpu.SMEM)
ANY = pl.BlockSpec(memory_space=pl.ANY)
F32, BF16 = jnp.float32, jnp.bfloat16
NX, NZ, NC, NM = 4, 4, 2, 8
NK = NX * NZ
ROWS, COLS, HALF = 64, 512, 32
ORDER = NM * ROWS
SLOTS = 4
BLOCKS = 48
OWNERS = NK * NC
EXTRAS = BLOCKS - OWNERS
FAR_FIRST = (2, 1, 3)
SEMS = 256
PLACE_OF, OCCUPIED, EXTRA_OF, MINE_OF, TABLE = 48, 96, 100, 104, 128


def dp_of(x, z, c):
    return {"dp": (x * NZ + z) * NC + c}


def device_of(x, z, c, j):
    return {"dp": (x * NZ + z) * NC + c, "mp": j}


def total(*parts):
    value = parts[0].astype(F32)
    for part in parts[1:]:
        value = value + part.astype(F32)
    return value.astype(BF16)


def mm(a, b):
    return jnp.dot(a, b, preferred_element_type=F32)


class Wires:
    def __init__(self, send, recv):
        self.send, self.recv, self.used, self.sent = send, recv, 0, []

    def take(self, count):
        self.used += count
        assert self.used <= SEMS
        return self.used - count

    def make(self, src, dst, device, at_send, at_recv):
        return pltpu.make_async_remote_copy(
            src_ref=src, dst_ref=dst, send_sem=self.send.at[at_send], recv_sem=self.recv.at[at_recv],
            device_id=device, device_id_type=MESH,
        )

    def go(self, src, dst, device):
        at = self.take(1)
        copy = self.make(src, dst, device, at, at)
        copy.start()
        self.sent.append(copy)
        return copy


class RingReduce:
    def __init__(self, wires, acc, passed, came, x, to):
        self.wires, self.acc, self.passed, self.came, self.x, self.to = wires, acc, passed, came, x, to
        self.right, self.left, self.far = (x + 1) % NX, (x + 3) % NX, (x + 2) % NX

    def part(self, at, h):
        return self.acc.at[pl.ds(at * NZ + 2 * h, 2)]

    def send_far(self):
        self.a = self.wires.go(self.part(self.far, 0), self.passed.at[0], self.to(self.right))
        self.b = self.wires.go(self.part(self.far, 1), self.passed.at[1], self.to(self.left))

    def send_right(self):
        self.c = self.wires.go(self.part(self.right, 1), self.came.at[0, pl.ds(2, 2)], self.to(self.right))

    def send_left(self):
        self.d = self.wires.go(self.part(self.left, 0), self.came.at[1, pl.ds(0, 2)], self.to(self.left))

    def forward(self):
        self.a.wait_recv()
        for q in range(2):
            at = self.right * NZ + q
            self.acc[at] = total(self.acc[at], self.passed[0, q])
        self.e = self.wires.go(self.part(self.right, 0), self.came.at[0, pl.ds(0, 2)], self.to(self.right))
        self.b.wait_recv()
        for q in range(2):
            at = self.left * NZ + 2 + q
            self.acc[at] = total(self.acc[at], self.passed[1, q])
        self.f = self.wires.go(self.part(self.left, 1), self.came.at[1, pl.ds(2, 2)], self.to(self.left))

    def finish(self, out):
        for copy in (self.c, self.d, self.e, self.f):
            copy.wait_recv()
        for q in range(NZ):
            out[q] = total(self.acc[self.x * NZ + q], self.came[0, q], self.came[1, q])


class RingGather:
    def __init__(self, wires, part, x, to):
        self.wires, self.part = wires, part
        self.x, self.right, self.left = x, (x + 1) % NX, (x + 3) % NX
        self.to_right, self.to_left = to(self.right), to(self.left)

    def push(self, at, h, device):
        return self.wires.go(self.part(at, h), self.part(at, h), device)

    def start(self):
        self.a = self.push(self.x, 0, self.to_right)
        self.b = self.push(self.x, 1, self.to_left)
        self.c = self.push(self.x, 1, self.to_right)
        self.d = self.push(self.x, 0, self.to_left)

    def forward(self):
        self.a.wait_recv()
        self.e = self.push(self.left, 0, self.to_right)
        self.b.wait_recv()
        self.f = self.push(self.right, 1, self.to_left)

    def finish_near(self):
        self.c.wait_recv()
        self.d.wait_recv()

    def finish_far(self):
        self.e.wait_recv()
        self.f.wait_recv()


def kernel(
    table, grads, left, right, first, second,
    all_out, left_hbm, right_hbm, first_hbm, second_hbm,
    gv, lv, rv, fv, sv, all_of, left_out, right_out, first_out, second_out,
    send_f, send_e, recv_f, recv_e, acc_f, acc_e, pass_f, pass_e, came_f, came_e, sum_f, sum_e,
    from_z_f, from_z_e, ext, own,
    grad, stat, norms, norms_in, mat, term, terms, power, factor, current, root, half, half_in, turned, update,
    send_d, recv_d, acc_d, pass_d, came_d, sum_d, from_z_d,
    send_sem, recv_sem, load_sem, store_sem,
):
    me = lax.axis_index("dp")
    j = lax.axis_index("mp")
    x, z, c = me // (NZ * NC), (me // NC) % NZ, me % NC
    y, zl = j // 2, j % 2
    other = 1 - c
    core = dp_of(x, z, other)
    to_x = lambda at: dp_of(at, z, c)
    w = Wires(send_sem, recv_sem)
    my_rows = pl.ds(j * ROWS, ROWS)
    lanes = lax.broadcasted_iota(jnp.int32, (ROWS, 128), 1)
    lines = lax.broadcasted_iota(jnp.int32, (ROWS, 128), 0)

    loads = [
        pltpu.make_async_copy(src, dst, load_sem.at[i])
        for i, (src, dst) in enumerate(((grads, gv), (left, lv), (right, rv), (first, fv), (second, sv)))
    ]
    for copy in loads:
        copy.start()

    barrier = pltpu.get_barrier_semaphore()
    greeted = 0
    for k in range(1, 4):
        for device in (dp_of((x + k) % NX, z, c), dp_of(x, (z + k) % NZ, c)):
            pl.semaphore_signal(barrier, inc=1, device_id=device, device_id_type=MESH)
            greeted += 1
    for k in range(NM):
        for which in range(NC):
            if k or which:
                device = device_of(x, z, (c + which) % NC, (j + k) % NM)
                pl.semaphore_signal(barrier, inc=1, device_id=device, device_id_type=MESH)
                greeted += 1
    pl.semaphore_wait(barrier, greeted)

    stat_send, stat_recv = w.take(2 * SLOTS), w.take(NM)
    stat_copies = []
    for s in range(SLOTS):
        for role, source in enumerate((left, right)):
            copy = w.make(
                source.at[s], stat.at[my_rows], device_of(x, z, role, 2 * s + c), stat_send + 2 * s + role,
                stat_recv + j,
            )
            here = (c == role) & (j == 2 * s + c)
            stat_copies.append((here, copy))

    def send_stats(slots):
        for here, copy in [stat_copies[2 * s + role] for s in slots for role in range(NC)]:

            @pl.when(jnp.logical_not(here))
            def _():
                copy.start()

    send_stats((0, 1))

    loads[0].wait()
    for k in range(NK):
        send_e[k] = gv[table[OWNERS + k], pl.ds(other * HALF, HALF)]
    core_e = w.go(send_e, recv_e, core)
    turns = (2, 1, 3, 0)
    core_f = []
    for k in turns:
        at = (x + k) % NX
        for q in range(NZ):
            send_f[at * NZ + q] = gv[table[(at * NZ + q) * NC + other]]
        rows = pl.ds(at * NZ, NZ)
        core_f.append(w.go(send_f.at[rows], recv_f.at[rows], core))

    ring_e = RingReduce(w, acc_e, pass_e, came_e, x, to_x)
    ring_f = RingReduce(w, acc_f, pass_f, came_f, x, to_x)
    core_e.wait_recv()

    def add_e(step):
        for q in range(NZ):
            k = ((x + turns[step]) % NX) * NZ + q
            acc_e[k] = total(gv[table[OWNERS + k], pl.ds(c * HALF, HALF)], recv_e[k])

    add_e(0)
    ring_e.send_far()
    add_e(1)
    ring_e.send_right()
    add_e(2)
    ring_e.send_left()
    add_e(3)

    def add_f(step):
        at = (x + turns[step]) % NX
        core_f[step].wait_recv()
        for q in range(NZ):
            acc_f[at * NZ + q] = total(gv[table[(at * NZ + q) * NC + c]], recv_f[at * NZ + q])

    loads[1].wait()
    loads[2].wait()
    for s in range(SLOTS):
        for role, source in enumerate((lv, rv)):

            @pl.when((c == role) & (j == 2 * s + c))
            def _():
                stat[my_rows] = source[s]

    add_f(0)
    ring_e.forward()
    ring_f.send_far()
    add_f(1)
    ring_f.send_right()
    add_f(2)
    ring_f.send_left()
    add_f(3)
    ring_e.finish(sum_e)
    z_e = [w.go(sum_e.at[(z + k) % NZ], from_z_e.at[k - 1], dp_of(x, (z + k) % NZ, c)) for k in FAR_FIRST]
    ring_f.forward()
    for copy in z_e:
        copy.wait_recv()
    mine = ext.at[x * NZ + z, pl.ds(c * HALF, HALF)]
    ext[x * NZ + z, pl.ds(c * HALF, HALF)] = total(sum_e[z], from_z_e[0], from_z_e[1], from_z_e[2])
    z_g = [w.go(mine, mine, dp_of(x, (z + k) % NZ, c)) for k in FAR_FIRST]

    def spread(ref, base, zs):
        def ring_of(k):
            at_z = (z + NZ - k) % NZ
            part = lambda at, h: ref.at[base + at * NZ + at_z, pl.ds(c * HALF + h * 16, 16)]
            return RingGather(w, part, x, to_x)

        line = lambda at: ref.at[pl.ds(base + at * NZ, NZ), pl.ds(c * HALF, HALF)]
        rings = {k: ring_of(k) for k in range(NZ)}
        rings[0].start()

        def rest(meanwhile):
            for k in (1, 3, 2):
                zs[FAR_FIRST.index(k)].wait_recv()
                rings[k].start()
            across = [w.go(line(x), line(x), core)]
            meanwhile()
            for k in (0, 1, 3, 2):
                rings[k].forward()
            for k in range(NZ):
                rings[k].finish_near()
            for at in ((x + 3) % NX, (x + 1) % NX):
                across.append(w.go(line(at), line(at), core))
            for k in range(NZ):
                rings[k].finish_far()
            far = (x + 2) % NX
            across.append(w.go(line(far), line(far), core))
            return across

        return rest

    spread_rest = spread(ext, 0, z_g)
    ring_f.finish(sum_f)
    z_f = [w.go(sum_f.at[(z + k) % NZ], from_z_f.at[k - 1], dp_of(x, (z + k) % NZ, c)) for k in FAR_FIRST]
    ext_core = spread_rest(lambda: send_stats((2, 3)))
    for copy in z_f:
        copy.wait_recv()
    own[0] = total(sum_f[z], from_z_f[0], from_z_f[1], from_z_f[2])

    g_send, g_recv, g_core = w.take(SLOTS), w.take(NM), w.take(NM)
    g_copies = [
        w.make(own.at[s], grad.at[my_rows], {"mp": 2 * s + c}, g_send + s, g_recv + j) for s in range(SLOTS)
    ]
    primary = c == zl

    def send_g(s):
        @pl.when(j != 2 * s + c)
        def _():
            g_copies[s].start()

        @pl.when(j == 2 * s + c)
        def _():
            grad[my_rows] = own[s]

    send_g(0)
    for copy in ext_core:
        copy.wait_recv()
    for s in range(1, SLOTS):
        own[s] = ext[table[EXTRA_OF + s]]
        send_g(s)

    stores = []

    def store(src, dst):
        copy = pltpu.make_async_copy(src, dst, store_sem.at[len(stores)])
        copy.start()
        stores.append(copy)

    loads[3].wait()
    loads[4].wait()
    n_send, n_recv = w.take(SLOTS), w.take(NM)
    n_copies = []
    for s in range(SLOTS):
        held = jnp.full((ROWS, COLS), table[OCCUPIED + s]) > 0
        g = own[s].astype(F32)
        m = 0.9 * fv[s] + 0.1 * g
        v = 0.95 * sv[s] + 0.05 * g * g
        first_out[s] = jnp.where(held, m, fv[s])
        second_out[s] = jnp.where(held, v, sv[s])
        a = m / (jnp.sqrt(v) + 1e-8)
        length = jnp.broadcast_to(jnp.sqrt(jnp.sum(a * a, axis=1, keepdims=True)), (ROWS, 128))
        length = jnp.sum(jnp.where(lanes == lines, length, 0.0), axis=0, keepdims=True)
        norms[s] = jnp.broadcast_to(length, (8, 128))
        copy = w.make(norms.at[s], norms_in.at[j], device_of(x, z, 1, 2 * s + c), n_send + s, n_recv + j)
        here = (c == 1) & (j == 2 * s + c)
        n_copies.append((here, copy))

        @pl.when(jnp.logical_not(here))
        def _():
            copy.start()

        @pl.when(here)
        def _():
            norms_in[j] = norms[s]

    store(first_out, first_hbm)
    store(second_out, second_hbm)
    handed = [
        w.make(grad.at[pl.ds(i * ROWS, ROWS)], grad.at[pl.ds(i * ROWS, ROWS)], core, g_core + i, g_core + i)
        for i in range(NM)
    ]

    @pl.when(primary)
    def _():
        for i in range(NM):

            @pl.when(j != i)
            def _():
                w.make(own.at[0], grad.at[pl.ds(i * ROWS, ROWS)], core, g_send, g_recv + i).wait_recv()

            handed[i].start()

    @pl.when(jnp.logical_not(primary))
    def _():
        for i in range(NM):
            handed[i].wait_recv()

    @pl.when(c == 0)
    def _():
        g = grad[...]
        mat[...] = lax.dot_general(g, g, (((1,), (1,)), ((), ())), preferred_element_type=F32)

    @pl.when(c == 1)
    def _():
        g = grad[...]
        mat[...] = lax.dot_general(g, g, (((0,), (0,)), ((), ())), preferred_element_type=F32)

    for i in range(NM):

        @pl.when(jnp.logical_not((zl == c) & (j == i)))
        def _():
            w.make(lv.at[0], stat.at[pl.ds(i * ROWS, ROWS)], core, stat_send, stat_recv + i).wait_recv()

    term[...] = mat[...].astype(BF16)
    t_send, t_recv = w.take(NM), w.take(2 * SLOTS)
    t_copies = []
    for i in range(NM):
        copy = w.make(
            term.at[pl.ds(i * ROWS, ROWS)], terms.at[c, y], device_of(x, z, zl, i), t_send + i,
            t_recv + c * SLOTS + y,
        )
        here = (zl == c) & (j == i)
        t_copies.append((here, copy))

        @pl.when(jnp.logical_not(here))
        def _():
            copy.start()

        @pl.when(here)
        def _():
            terms[c, y] = term[pl.ds(i * ROWS, ROWS)]

    whole = 0.9 * stat[...] + 0.1 * mat[...]
    mat[...] = whole
    frobenius = jnp.sqrt(jnp.sum(whole * whole, keepdims=True))
    scaling = 5.0 / (2.0 * frobenius)
    start = jnp.sqrt(jnp.sqrt(scaling)).astype(BF16).astype(F32)
    diagonal = lax.broadcasted_iota(jnp.int32, (ORDER, ORDER), 0) == lax.broadcasted_iota(
        jnp.int32, (ORDER, ORDER), 1
    )
    five = jnp.where(diagonal, 5.0, 0.0).astype(F32)
    current[...] = (scaling * mat[...]).astype(BF16)
    factor[...] = ((five - current[...].astype(F32)) * 0.25).astype(BF16)
    root[...] = (start * factor[...].astype(F32)).astype(BF16)

    def sweep(_, carry):
        power[...] = mm(factor[...], factor[...]).astype(BF16)
        power[...] = mm(power[...], power[...]).astype(BF16)
        current[...] = mm(power[...], current[...]).astype(BF16)
        factor[...] = ((five - current[...].astype(F32)) * 0.25).astype(BF16)
        root[...] = mm(root[...], factor[...]).astype(BF16)
        return carry

    lax.fori_loop(0, ITERS - 1, sweep, 0)

    step = 2 * ROWS
    count = ORDER // step
    h_at = w.take(count)
    h_copies = [
        w.make(half.at[pl.ds(i * step, step)], half_in.at[pl.ds(i * step, step)], core, h_at + i, h_at + i)
        for i in range(count)
    ]
    d_send, d_recv = w.take(NM), w.take(SLOTS)
    d_copies = [
        w.make(
            turned.at[pl.ds(i * ROWS, ROWS)], update.at[y], device_of(x, z, zl, i), d_send + i, d_recv + y
        )
        for i in range(NM)
    ]

    @pl.when(c == 0)
    def _():
        for i in range(count):
            rows = pl.ds(i * step, step)
            half[rows] = mm(root[rows], grad[...]).astype(BF16)
            h_copies[i].start()

    @pl.when(c == 1)
    def _():
        for i in range(NM):

            @pl.when(jnp.logical_not((zl == 1) & (j == i)))
            def _():
                w.make(norms.at[0], norms_in.at[i], core, n_send, n_recv + i).wait_recv()

        for i in range(count):
            rows = pl.ds(i * step, step)
            h_copies[i].wait_recv()
            s = mm(half_in[rows], root[...])
            for u in range(2):
                to = 2 * i + u
                here = (zl == 1) & (j == to)
                piece = s[u * ROWS : (u + 1) * ROWS]
                length = jnp.sqrt(jnp.sum(piece * piece, axis=1, keepdims=True)) + 1e-6
                adam = jnp.broadcast_to(norms_in[to, 0:1], (ROWS, 128))
                adam = jnp.sum(jnp.where(lanes == lines, adam, 0.0), axis=1, keepdims=True)
                turned[pl.ds(to * ROWS, ROWS)] = (piece * (adam / length)).astype(BF16)

                @pl.when(jnp.logical_not(here))
                def _():
                    d_copies[to].start()

                @pl.when(here)
                def _():
                    update[y] = turned[pl.ds(to * ROWS, ROWS)]

    def wait_update(s):
        @pl.when(jnp.logical_not((c == 1) & (j == 2 * s + c)))
        def _():
            w.make(turned.at[pl.ds(0, ROWS)], update.at[s], core, d_send, d_recv + s).wait_recv()

    here_f = c * NK + x * NZ + z
    wait_update(0)
    all_of[here_f] = update[0]
    f_z = [w.go(all_of.at[here_f], all_of.at[here_f], dp_of(x, (z + k) % NZ, c)) for k in FAR_FIRST]

    def ring_of(k):
        at_z = (z + NZ - k) % NZ
        part = lambda at, h: all_of.at[c * NK + at * NZ + at_z, pl.ds(h * HALF, HALF)]
        return RingGather(w, part, x, to_x)

    rings = {k: ring_of(k) for k in range(NZ)}
    for q in range(1, SLOTS):
        wait_update(q)

    def picked(e, which):
        at = table[MINE_OF + e]
        value = update[at, pl.ds(which * HALF, HALF)]
        return jnp.where(jnp.full(value.shape, at) > 0, value.astype(F32), 0.0)

    for e in range(EXTRAS):
        send_d[e] = picked(e, other).astype(BF16)
    core_d = w.go(send_d, recv_d, core)
    ring_d = RingReduce(w, acc_d, pass_d, came_d, x, to_x)
    core_d.wait_recv()
    for k, send in ((2, ring_d.send_far), (1, ring_d.send_right), (3, ring_d.send_left), (0, None)):
        for q in range(NZ):
            e = ((x + k) % NX) * NZ + q
            acc_d[e] = (picked(e, c) + recv_d[e].astype(F32)).astype(BF16)
        if send:
            send()
    ring_d.forward()
    rings[0].start()
    ring_d.finish(sum_d)
    z_d = [w.go(sum_d.at[(z + k) % NZ], from_z_d.at[k - 1], dp_of(x, (z + k) % NZ, c)) for k in FAR_FIRST]
    for copy, k in sorted(zip(f_z, FAR_FIRST), key=lambda pair: pair[1] == 2):
        copy.wait_recv()
        rings[k].start()
    f_line = lambda at: all_of.at[pl.ds(c * NK + at * NZ, NZ)]
    f_core = [w.go(f_line(x), f_line(x), core)]
    rings[0].forward()
    for copy in z_d:
        copy.wait_recv()
    here_e = (OWNERS + x * NZ + z, pl.ds(c * HALF, HALF))
    all_of[here_e] = total(sum_d[z], from_z_d[0], from_z_d[1], from_z_d[2])
    mine = all_of.at[here_e]
    z_g = [w.go(mine, mine, dp_of(x, (z + k) % NZ, c)) for k in FAR_FIRST]
    spread_rest = spread(all_of, OWNERS, z_g)
    for k in (1, 3, 2):
        rings[k].forward()

    for role in range(2):
        for s in range(SLOTS):

            @pl.when(jnp.logical_not((role == c) & (j == 2 * s + c)))
            def _():
                w.make(
                    term.at[pl.ds(0, ROWS)], terms.at[role, s], core, t_send, t_recv + role * SLOTS + s
                ).wait_recv()

            old, new = ((lv, left_out), (rv, right_out))[role]
            held = jnp.full((ROWS, COLS), table[OCCUPIED + s]) > 0
            new[s] = jnp.where(held, 0.9 * old[s] + 0.1 * terms[role, s].astype(F32), old[s])

    store(left_out, left_hbm)
    store(right_out, right_hbm)
    for k in range(NZ):
        rings[k].finish_near()
    for at in ((x + 3) % NX, (x + 1) % NX):
        f_core.append(w.go(f_line(at), f_line(at), core))
    e_core = spread_rest(lambda: None)
    for k in range(NZ):
        rings[k].finish_far()
    f_core.append(w.go(f_line((x + 2) % NX), f_line((x + 2) % NX), core))
    for copy in f_core:
        copy.wait_recv()
    firsts = pl.ds(0, OWNERS)
    store(all_of.at[firsts], all_out.at[firsts])
    for copy in e_core:
        copy.wait_recv()
    extras = pl.ds(OWNERS, EXTRAS)
    store(all_of.at[extras], all_out.at[extras])

    for copy in stores:
        copy.wait()
    for copy in w.sent:
        copy.wait_send()
    for here, copy in stat_copies + n_copies + t_copies:

        @pl.when(jnp.logical_not(here))
        def _():
            copy.wait_send()

    for s in range(SLOTS):

        @pl.when(j != 2 * s + c)
        def _():
            g_copies[s].wait_send()

    @pl.when(primary)
    def _():
        for copy in handed:
            copy.wait_send()

    @pl.when(c == 0)
    def _():
        for copy in h_copies:
            copy.wait_send()

    @pl.when(c == 1)
    def _():
        for i in range(NM):

            @pl.when(jnp.logical_not((zl == 1) & (j == i)))
            def _():
                d_copies[i].wait_send()


def whole_step(table, grads, left, right, first, second):
    state = jax.ShapeDtypeStruct((SLOTS, ROWS, COLS), F32)
    v = lambda *shape, kind=BF16: pltpu.VMEM(shape, kind)
    dma = pltpu.SemaphoreType.DMA
    half = (HALF, COLS)
    full = (ROWS, COLS)
    return pl.pallas_call(
        kernel,
        out_shape=(jax.ShapeDtypeStruct((BLOCKS, ROWS, COLS), BF16), state, state, state, state),
        in_specs=[SMEM] + [ANY] * 5,
        out_specs=(ANY,) * 5,
        scratch_shapes=[v(BLOCKS, *full)]
        + [v(SLOTS, *full, kind=F32)] * 4
        + [v(BLOCKS, *full)]
        + [v(SLOTS, *full, kind=F32)] * 4
        + [
            v(NK, *full), v(NK, *half), v(NK, *full), v(NK, *half), v(NK, *full), v(NK, *half),
            v(2, 2, *full), v(2, 2, *half), v(2, NZ, *full), v(2, NZ, *half), v(NZ, *full), v(NZ, *half),
            v(3, *full), v(3, *half), v(EXTRAS, *full), v(SLOTS, *full),
        ]
        + [
            v(ORDER, COLS), v(ORDER, COLS, kind=F32), v(SLOTS, 8, 128, kind=F32), v(NM, 8, 128, kind=F32),
            v(ORDER, COLS, kind=F32), v(ORDER, COLS), v(2, SLOTS, *full),
        ]
        + [v(ORDER, COLS)] * 7
        + [v(SLOTS, *full)]
        + [
            v(EXTRAS, *half), v(EXTRAS, *half), v(EXTRAS, *half), v(2, 2, *half),
            v(2, NZ, *half), v(NZ, *half), v(3, *half),
        ]
        + [dma((SEMS,)), dma((SEMS,)), dma((5,)), dma((7,))],
        compiler_params=pltpu.CompilerParams(
            collective_id=0, has_side_effects=True, vmem_limit_bytes=56 << 20
        ),
        name="shampoo_step",
    )(table, grads, left, right, first, second)


def table_kernel(owner, table, counts):
    me = lax.axis_index("dp")

    def clear(i, carry):
        table[i] = 0
        return carry

    def clear_counts(i, carry):
        counts[i] = 0
        return carry

    lax.fori_loop(OCCUPIED, MINE_OF + EXTRAS, clear, 0)
    lax.fori_loop(0, OWNERS, clear_counts, 0)

    def visit(b, rank):
        o = owner[b]
        slot = counts[o]
        counts[o] = slot + 1
        again = slot > 0
        table[jnp.where(again, OWNERS + rank, o)] = b
        table[PLACE_OF + b] = jnp.where(again, OWNERS + rank, (o % NC) * NK + o // NC)

        @pl.when(o == me)
        def _():
            table[OCCUPIED + slot] = 1

            @pl.when(again)
            def _():
                table[EXTRA_OF + slot] = rank
                table[MINE_OF + rank] = slot

        return rank + again.astype(jnp.int32)

    lax.fori_loop(0, BLOCKS, visit, jnp.int32(0))


def tables(owners):
    return pl.pallas_call(
        table_kernel,
        out_shape=jax.ShapeDtypeStruct((TABLE,), jnp.int32),
        in_specs=[SMEM],
        out_specs=SMEM,
        scratch_shapes=[pltpu.SMEM((OWNERS,), jnp.int32)],
        name="tables",
    )(owners[:, 0])


def output_kernel(
    table, all_of, a, b, c, d, out, a_out, b_out, c_out, d_out, held, a_held, b_held, c_held, d_held, came, sent
):
    load = pltpu.make_async_copy(all_of, held, came.at[0])
    load.start()
    states = ((a, a_held, a_out), (b, b_held, b_out), (c, c_held, c_out), (d, d_held, d_out))
    ins = [pltpu.make_async_copy(src, mid, came.at[1 + i]) for i, (src, mid, _) in enumerate(states)]
    outs = [pltpu.make_async_copy(mid, dst.at[0], sent.at[1 + i]) for i, (_, mid, dst) in enumerate(states)]
    for copy in ins:
        copy.start()
    load.wait()
    for i in range(BLOCKS):
        pltpu.make_async_copy(held.at[table[PLACE_OF + i]], out.at[i], sent.at[0]).start()
    for copy_in, copy_out in zip(ins, outs):
        copy_in.wait()
        copy_out.start()
    pltpu.make_async_copy(held, out, sent.at[0]).wait()
    for copy in outs:
        copy.wait()


def outputs(table, *parts):
    state = jax.ShapeDtypeStruct((1, SLOTS, ROWS, COLS), F32)
    return pl.pallas_call(
        output_kernel,
        out_shape=(jax.ShapeDtypeStruct((BLOCKS, ROWS, COLS), BF16), state, state, state, state),
        in_specs=[SMEM] + [ANY] * 5,
        out_specs=(ANY,) * 5,
        scratch_shapes=[pltpu.VMEM((BLOCKS, ROWS, COLS), BF16)]
        + [pltpu.VMEM((SLOTS, ROWS, COLS), F32)] * 4
        + [pltpu.SemaphoreType.DMA((5,))] * 2,
        compiler_params=pltpu.CompilerParams(vmem_limit_bytes=56 << 20),
        name="outputs",
    )(table, *parts)


def body(grads, owners, left_stat, right_stat, first_moment, second_moment):
    table = tables(owners)
    parts = whole_step(table, grads[0], left_stat[0], right_stat[0], first_moment[0], second_moment[0])
    return outputs(table, *parts)


def solution(mesh):
    split = P("dp", None, "mp", None)
    return jax.shard_map(
        body,
        mesh=mesh,
        in_specs=(split, P(), split, split, split, split),
        out_specs=(P(None, "mp", None), split, split, split, split),
        check_vma=False,
    )
```

```python
import jax
import jax.numpy as jnp
from jax import lax
from jax.experimental import pallas as pl
from jax.experimental.pallas import tpu as pltpu
from jax.sharding import PartitionSpec as P

ITERS = 6
MESH = pl.DeviceIdType.MESH
VMEM = pl.BlockSpec(memory_space=pltpu.VMEM)
SMEM = pl.BlockSpec(memory_space=pltpu.SMEM)
ANY = pl.BlockSpec(memory_space=pl.ANY)
F32, BF16 = jnp.float32, jnp.bfloat16
NX, NZ, NC, NM = 4, 4, 2, 8
NK = NX * NZ
ROWS, COLS, HALF = 64, 512, 32
ORDER = NM * ROWS
SLOTS = 4
BLOCKS = 48
OWNERS = NK * NC
EXTRAS = BLOCKS - OWNERS
FAR_FIRST = (2, 1, 3)
SEMS = 256
PLACE_OF, OCCUPIED, EXTRA_OF, MINE_OF, TABLE = 48, 96, 100, 104, 128


def dp_of(x, z, c):
    return {"dp": (x * NZ + z) * NC + c}


def device_of(x, z, c, j):
    return {"dp": (x * NZ + z) * NC + c, "mp": j}


def total(*parts):
    value = parts[0].astype(F32)
    for part in parts[1:]:
        value = value + part.astype(F32)
    return value.astype(BF16)


def mm(a, b):
    return jnp.dot(a, b, preferred_element_type=F32)


class Wires:
    def __init__(self, send, recv):
        self.send, self.recv, self.used, self.sent = send, recv, 0, []

    def take(self, count):
        self.used += count
        assert self.used <= SEMS
        return self.used - count

    def make(self, src, dst, device, at_send, at_recv):
        return pltpu.make_async_remote_copy(
            src_ref=src, dst_ref=dst, send_sem=self.send.at[at_send], recv_sem=self.recv.at[at_recv],
            device_id=device, device_id_type=MESH,
        )

    def go(self, src, dst, device):
        at = self.take(1)
        copy = self.make(src, dst, device, at, at)
        copy.start()
        self.sent.append(copy)
        return copy


class RingReduce:
    def __init__(self, wires, acc, passed, came, x, to):
        self.wires, self.acc, self.passed, self.came, self.x, self.to = wires, acc, passed, came, x, to
        self.right, self.left, self.far = (x + 1) % NX, (x + 3) % NX, (x + 2) % NX

    def part(self, at, h):
        return self.acc.at[pl.ds(at * NZ + 2 * h, 2)]

    def send_far(self):
        self.a = self.wires.go(self.part(self.far, 0), self.passed.at[0], self.to(self.right))
        self.b = self.wires.go(self.part(self.far, 1), self.passed.at[1], self.to(self.left))

    def send_right(self):
        self.c = self.wires.go(self.part(self.right, 1), self.came.at[0, pl.ds(2, 2)], self.to(self.right))

    def send_left(self):
        self.d = self.wires.go(self.part(self.left, 0), self.came.at[1, pl.ds(0, 2)], self.to(self.left))

    def forward(self):
        self.a.wait_recv()
        for q in range(2):
            at = self.right * NZ + q
            self.acc[at] = total(self.acc[at], self.passed[0, q])
        self.e = self.wires.go(self.part(self.right, 0), self.came.at[0, pl.ds(0, 2)], self.to(self.right))
        self.b.wait_recv()
        for q in range(2):
            at = self.left * NZ + 2 + q
            self.acc[at] = total(self.acc[at], self.passed[1, q])
        self.f = self.wires.go(self.part(self.left, 1), self.came.at[1, pl.ds(2, 2)], self.to(self.left))

    def finish(self, out):
        for copy in (self.c, self.d, self.e, self.f):
            copy.wait_recv()
        for q in range(NZ):
            out[q] = total(self.acc[self.x * NZ + q], self.came[0, q], self.came[1, q])


class RingGather:
    def __init__(self, wires, part, x, to):
        self.wires, self.part = wires, part
        self.x, self.right, self.left = x, (x + 1) % NX, (x + 3) % NX
        self.to_right, self.to_left = to(self.right), to(self.left)

    def push(self, at, h, device):
        return self.wires.go(self.part(at, h), self.part(at, h), device)

    def start(self):
        self.a = self.push(self.x, 0, self.to_right)
        self.b = self.push(self.x, 1, self.to_left)
        self.c = self.push(self.x, 1, self.to_right)
        self.d = self.push(self.x, 0, self.to_left)

    def forward(self):
        self.a.wait_recv()
        self.e = self.push(self.left, 0, self.to_right)
        self.b.wait_recv()
        self.f = self.push(self.right, 1, self.to_left)

    def finish_near(self):
        self.c.wait_recv()
        self.d.wait_recv()

    def finish_far(self):
        self.e.wait_recv()
        self.f.wait_recv()


def kernel(
    table, grads, left, right, first, second,
    all_out, left_hbm, right_hbm, first_hbm, second_hbm,
    gv, lv, rv, fv, sv, all_of, left_out, right_out, first_out, second_out,
    send_f, send_e, recv_f, recv_e, acc_f, acc_e, pass_f, pass_e, came_f, came_e, sum_f, sum_e,
    from_z_f, from_z_e, ext, own,
    grad, stat, norms, norms_in, mat, term, terms, power, factor, current, root, half, half_in, turned, update,
    send_d, recv_d, acc_d, pass_d, came_d, sum_d, from_z_d,
    send_sem, recv_sem, load_sem, store_sem,
):
    me = lax.axis_index("dp")
    j = lax.axis_index("mp")
    x, z, c = me // (NZ * NC), (me // NC) % NZ, me % NC
    y, zl = j // 2, j % 2
    other = 1 - c
    core = dp_of(x, z, other)
    to_x = lambda at: dp_of(at, z, c)
    w = Wires(send_sem, recv_sem)
    my_rows = pl.ds(j * ROWS, ROWS)
    lanes = lax.broadcasted_iota(jnp.int32, (ROWS, 128), 1)
    lines = lax.broadcasted_iota(jnp.int32, (ROWS, 128), 0)

    loads = [
        pltpu.make_async_copy(src, dst, load_sem.at[i])
        for i, (src, dst) in enumerate(((grads, gv), (left, lv), (right, rv), (first, fv), (second, sv)))
    ]
    for copy in loads:
        copy.start()

    barrier = pltpu.get_barrier_semaphore()
    greeted = 0
    for k in range(1, 4):
        for device in (dp_of((x + k) % NX, z, c), dp_of(x, (z + k) % NZ, c)):
            pl.semaphore_signal(barrier, inc=1, device_id=device, device_id_type=MESH)
            greeted += 1
    for k in range(NM):
        for which in range(NC):
            if k or which:
                device = device_of(x, z, (c + which) % NC, (j + k) % NM)
                pl.semaphore_signal(barrier, inc=1, device_id=device, device_id_type=MESH)
                greeted += 1
    pl.semaphore_wait(barrier, greeted)

    stat_send, stat_recv = w.take(2 * SLOTS), w.take(NM)
    stat_copies = []
    for s in range(SLOTS):
        for role, source in enumerate((left, right)):
            copy = w.make(
                source.at[s], stat.at[my_rows], device_of(x, z, role, 2 * s + c), stat_send + 2 * s + role,
                stat_recv + j,
            )
            here = (c == role) & (j == 2 * s + c)
            stat_copies.append((here, copy))

    def send_stats(slots):
        for here, copy in [stat_copies[2 * s + role] for s in slots for role in range(NC)]:

            @pl.when(jnp.logical_not(here))
            def _():
                copy.start()

    send_stats((0, 1))

    loads[0].wait()
    for k in range(NK):
        send_e[k] = gv[table[OWNERS + k], pl.ds(other * HALF, HALF)]
    core_e = w.go(send_e, recv_e, core)
    turns = (2, 1, 3, 0)
    core_f = []
    for k in turns:
        at = (x + k) % NX
        for q in range(NZ):
            send_f[at * NZ + q] = gv[table[(at * NZ + q) * NC + other]]
        rows = pl.ds(at * NZ, NZ)
        core_f.append(w.go(send_f.at[rows], recv_f.at[rows], core))

    ring_e = RingReduce(w, acc_e, pass_e, came_e, x, to_x)
    ring_f = RingReduce(w, acc_f, pass_f, came_f, x, to_x)
    core_e.wait_recv()

    def add_e(step):
        for q in range(NZ):
            k = ((x + turns[step]) % NX) * NZ + q
            acc_e[k] = total(gv[table[OWNERS + k], pl.ds(c * HALF, HALF)], recv_e[k])

    add_e(0)
    ring_e.send_far()
    add_e(1)
    ring_e.send_right()
    add_e(2)
    ring_e.send_left()
    add_e(3)

    def add_f(step):
        at = (x + turns[step]) % NX
        core_f[step].wait_recv()
        for q in range(NZ):
            acc_f[at * NZ + q] = total(gv[table[(at * NZ + q) * NC + c]], recv_f[at * NZ + q])

    loads[1].wait()
    loads[2].wait()
    for s in range(SLOTS):
        for role, source in enumerate((lv, rv)):

            @pl.when((c == role) & (j == 2 * s + c))
            def _():
                stat[my_rows] = source[s]

    add_f(0)
    ring_e.forward()
    ring_f.send_far()
    add_f(1)
    ring_f.send_right()
    add_f(2)
    ring_f.send_left()
    add_f(3)
    ring_e.finish(sum_e)
    z_e = [w.go(sum_e.at[(z + k) % NZ], from_z_e.at[k - 1], dp_of(x, (z + k) % NZ, c)) for k in FAR_FIRST]
    ring_f.forward()
    for copy in z_e:
        copy.wait_recv()
    mine = ext.at[x * NZ + z, pl.ds(c * HALF, HALF)]
    ext[x * NZ + z, pl.ds(c * HALF, HALF)] = total(sum_e[z], from_z_e[0], from_z_e[1], from_z_e[2])
    z_g = [w.go(mine, mine, dp_of(x, (z + k) % NZ, c)) for k in FAR_FIRST]

    def spread(ref, base, zs):
        def ring_of(k):
            at_z = (z + NZ - k) % NZ
            part = lambda at, h: ref.at[base + at * NZ + at_z, pl.ds(c * HALF + h * 16, 16)]
            return RingGather(w, part, x, to_x)

        line = lambda at: ref.at[pl.ds(base + at * NZ, NZ), pl.ds(c * HALF, HALF)]
        rings = {k: ring_of(k) for k in range(NZ)}
        rings[0].start()

        def rest(meanwhile):
            for k in (1, 3, 2):
                zs[FAR_FIRST.index(k)].wait_recv()
                rings[k].start()
            across = [w.go(line(x), line(x), core)]
            meanwhile()
            for k in (0, 1, 3, 2):
                rings[k].forward()
            for k in range(NZ):
                rings[k].finish_near()
            for at in ((x + 3) % NX, (x + 1) % NX):
                across.append(w.go(line(at), line(at), core))
            for k in range(NZ):
                rings[k].finish_far()
            far = (x + 2) % NX
            across.append(w.go(line(far), line(far), core))
            return across

        return rest

    spread_rest = spread(ext, 0, z_g)
    ring_f.finish(sum_f)
    z_f = []
    def then():
        for k in FAR_FIRST:
            at = (z + k) % NZ
            z_f.append(w.go(sum_f.at[at], from_z_f.at[k - 1], dp_of(x, at, c)))
        send_stats((2, 3))

    ext_core = spread_rest(then)
    for copy in z_f:
        copy.wait_recv()
    own[0] = total(sum_f[z], from_z_f[0], from_z_f[1], from_z_f[2])

    g_send, g_recv, g_core = w.take(SLOTS), w.take(NM), w.take(NM)
    g_copies = [
        w.make(own.at[s], grad.at[my_rows], {"mp": 2 * s + c}, g_send + s, g_recv + j) for s in range(SLOTS)
    ]
    primary = c == zl

    def send_g(s):
        @pl.when(j != 2 * s + c)
        def _():
            g_copies[s].start()

        @pl.when(j == 2 * s + c)
        def _():
            grad[my_rows] = own[s]

    send_g(0)
    for copy in ext_core:
        copy.wait_recv()
    for s in range(1, SLOTS):
        own[s] = ext[table[EXTRA_OF + s]]
        send_g(s)

    stores = []

    def store(src, dst):
        copy = pltpu.make_async_copy(src, dst, store_sem.at[len(stores)])
        copy.start()
        stores.append(copy)

    loads[3].wait()
    loads[4].wait()
    n_send, n_recv = w.take(SLOTS), w.take(NM)
    n_copies = []
    for s in range(SLOTS):
        held = jnp.full((ROWS, COLS), table[OCCUPIED + s]) > 0
        g = own[s].astype(F32)
        m = 0.9 * fv[s] + 0.1 * g
        v = 0.95 * sv[s] + 0.05 * g * g
        first_out[s] = jnp.where(held, m, fv[s])
        second_out[s] = jnp.where(held, v, sv[s])
        a = m / (jnp.sqrt(v) + 1e-8)
        length = jnp.broadcast_to(jnp.sqrt(jnp.sum(a * a, axis=1, keepdims=True)), (ROWS, 128))
        length = jnp.sum(jnp.where(lanes == lines, length, 0.0), axis=0, keepdims=True)
        norms[s] = jnp.broadcast_to(length, (8, 128))
        copy = w.make(norms.at[s], norms_in.at[j], device_of(x, z, 1, 2 * s + c), n_send + s, n_recv + j)
        here = (c == 1) & (j == 2 * s + c)
        n_copies.append((here, copy))

        @pl.when(jnp.logical_not(here))
        def _():
            copy.start()

        @pl.when(here)
        def _():
            norms_in[j] = norms[s]

    store(first_out, first_hbm)
    store(second_out, second_hbm)
    handed = [
        w.make(grad.at[pl.ds(i * ROWS, ROWS)], grad.at[pl.ds(i * ROWS, ROWS)], core, g_core + i, g_core + i)
        for i in range(NM)
    ]

    @pl.when(primary)
    def _():
        for i in range(NM):

            @pl.when(j != i)
            def _():
                w.make(own.at[0], grad.at[pl.ds(i * ROWS, ROWS)], core, g_send, g_recv + i).wait_recv()

            handed[i].start()

    @pl.when(jnp.logical_not(primary))
    def _():
        for i in range(NM):
            handed[i].wait_recv()

    @pl.when(c == 0)
    def _():
        g = grad[...]
        mat[...] = lax.dot_general(g, g, (((1,), (1,)), ((), ())), preferred_element_type=F32)

    @pl.when(c == 1)
    def _():
        g = grad[...]
        mat[...] = lax.dot_general(g, g, (((0,), (0,)), ((), ())), preferred_element_type=F32)

    for i in range(NM):

        @pl.when(jnp.logical_not((zl == c) & (j == i)))
        def _():
            w.make(lv.at[0], stat.at[pl.ds(i * ROWS, ROWS)], core, stat_send, stat_recv + i).wait_recv()

    term[...] = mat[...].astype(BF16)
    t_send, t_recv = w.take(NM), w.take(2 * SLOTS)
    t_copies = []
    for i in range(NM):
        copy = w.make(
            term.at[pl.ds(i * ROWS, ROWS)], terms.at[c, y], device_of(x, z, zl, i), t_send + i,
            t_recv + c * SLOTS + y,
        )
        here = (zl == c) & (j == i)
        t_copies.append((here, copy))

        @pl.when(jnp.logical_not(here))
        def _():
            copy.start()

        @pl.when(here)
        def _():
            terms[c, y] = term[pl.ds(i * ROWS, ROWS)]

    whole = 0.9 * stat[...] + 0.1 * mat[...]
    mat[...] = whole
    frobenius = jnp.sqrt(jnp.sum(whole * whole, keepdims=True))
    scaling = 5.0 / (2.0 * frobenius)
    start = jnp.sqrt(jnp.sqrt(scaling)).astype(BF16).astype(F32)
    diagonal = lax.broadcasted_iota(jnp.int32, (ORDER, ORDER), 0) == lax.broadcasted_iota(
        jnp.int32, (ORDER, ORDER), 1
    )
    five = jnp.where(diagonal, 5.0, 0.0).astype(F32)
    current[...] = (scaling * mat[...]).astype(BF16)
    factor[...] = ((five - current[...].astype(F32)) * 0.25).astype(BF16)
    root[...] = (start * factor[...].astype(F32)).astype(BF16)

    def sweep(_, carry):
        power[...] = mm(factor[...], factor[...]).astype(BF16)
        power[...] = mm(power[...], power[...]).astype(BF16)
        current[...] = mm(power[...], current[...]).astype(BF16)
        factor[...] = ((five - current[...].astype(F32)) * 0.25).astype(BF16)
        root[...] = mm(root[...], factor[...]).astype(BF16)
        return carry

    lax.fori_loop(0, ITERS - 1, sweep, 0)

    step = 2 * ROWS
    count = ORDER // step
    h_at = w.take(count)
    h_copies = [
        w.make(half.at[pl.ds(i * step, step)], half_in.at[pl.ds(i * step, step)], core, h_at + i, h_at + i)
        for i in range(count)
    ]
    d_send, d_recv = w.take(NM), w.take(SLOTS)
    d_copies = [
        w.make(
            turned.at[pl.ds(i * ROWS, ROWS)], update.at[y], device_of(x, z, zl, i), d_send + i, d_recv + y
        )
        for i in range(NM)
    ]

    @pl.when(c == 0)
    def _():
        for i in range(count):
            rows = pl.ds(i * step, step)
            half[rows] = mm(root[rows], grad[...]).astype(BF16)
            h_copies[i].start()

    @pl.when(c == 1)
    def _():
        for i in range(NM):

            @pl.when(jnp.logical_not((zl == 1) & (j == i)))
            def _():
                w.make(norms.at[0], norms_in.at[i], core, n_send, n_recv + i).wait_recv()

        for i in range(count):
            rows = pl.ds(i * step, step)
            h_copies[i].wait_recv()
            s = mm(half_in[rows], root[...])
            for u in range(2):
                to = 2 * i + u
                here = (zl == 1) & (j == to)
                piece = s[u * ROWS : (u + 1) * ROWS]
                length = jnp.sqrt(jnp.sum(piece * piece, axis=1, keepdims=True)) + 1e-6
                adam = jnp.broadcast_to(norms_in[to, 0:1], (ROWS, 128))
                adam = jnp.sum(jnp.where(lanes == lines, adam, 0.0), axis=1, keepdims=True)
                turned[pl.ds(to * ROWS, ROWS)] = (piece * (adam / length)).astype(BF16)

                @pl.when(jnp.logical_not(here))
                def _():
                    d_copies[to].start()

                @pl.when(here)
                def _():
                    update[y] = turned[pl.ds(to * ROWS, ROWS)]

    def wait_update(s):
        @pl.when(jnp.logical_not((c == 1) & (j == 2 * s + c)))
        def _():
            w.make(turned.at[pl.ds(0, ROWS)], update.at[s], core, d_send, d_recv + s).wait_recv()

    here_f = c * NK + x * NZ + z
    wait_update(0)
    all_of[here_f] = update[0]
    f_z = [w.go(all_of.at[here_f], all_of.at[here_f], dp_of(x, (z + k) % NZ, c)) for k in FAR_FIRST]

    def ring_of(k):
        at_z = (z + NZ - k) % NZ
        part = lambda at, h: all_of.at[c * NK + at * NZ + at_z, pl.ds(h * HALF, HALF)]
        return RingGather(w, part, x, to_x)

    rings = {k: ring_of(k) for k in range(NZ)}
    for q in range(1, SLOTS):
        wait_update(q)

    def picked(e, which):
        at = table[MINE_OF + e]
        value = update[at, pl.ds(which * HALF, HALF)]
        return jnp.where(jnp.full(value.shape, at) > 0, value.astype(F32), 0.0)

    for e in range(EXTRAS):
        send_d[e] = picked(e, other).astype(BF16)
    core_d = w.go(send_d, recv_d, core)
    ring_d = RingReduce(w, acc_d, pass_d, came_d, x, to_x)
    core_d.wait_recv()
    for k, send in ((2, ring_d.send_far), (1, ring_d.send_right), (3, ring_d.send_left), (0, None)):
        for q in range(NZ):
            e = ((x + k) % NX) * NZ + q
            acc_d[e] = (picked(e, c) + recv_d[e].astype(F32)).astype(BF16)
        if send:
            send()
    ring_d.forward()
    rings[0].start()
    ring_d.finish(sum_d)
    z_d = [w.go(sum_d.at[(z + k) % NZ], from_z_d.at[k - 1], dp_of(x, (z + k) % NZ, c)) for k in FAR_FIRST]
    for copy, k in sorted(zip(f_z, FAR_FIRST), key=lambda pair: pair[1] == 2):
        copy.wait_recv()
        rings[k].start()
    f_line = lambda at: all_of.at[pl.ds(c * NK + at * NZ, NZ)]
    f_core = [w.go(f_line(x), f_line(x), core)]
    rings[0].forward()
    for copy in z_d:
        copy.wait_recv()
    here_e = (OWNERS + x * NZ + z, pl.ds(c * HALF, HALF))
    all_of[here_e] = total(sum_d[z], from_z_d[0], from_z_d[1], from_z_d[2])
    mine = all_of.at[here_e]
    z_g = [w.go(mine, mine, dp_of(x, (z + k) % NZ, c)) for k in FAR_FIRST]
    spread_rest = spread(all_of, OWNERS, z_g)
    for k in (1, 3, 2):
        rings[k].forward()

    for role in range(2):
        for s in range(SLOTS):

            @pl.when(jnp.logical_not((role == c) & (j == 2 * s + c)))
            def _():
                w.make(
                    term.at[pl.ds(0, ROWS)], terms.at[role, s], core, t_send, t_recv + role * SLOTS + s
                ).wait_recv()

            old, new = ((lv, left_out), (rv, right_out))[role]
            held = jnp.full((ROWS, COLS), table[OCCUPIED + s]) > 0
            new[s] = jnp.where(held, 0.9 * old[s] + 0.1 * terms[role, s].astype(F32), old[s])

    store(left_out, left_hbm)
    store(right_out, right_hbm)
    for k in range(NZ):
        rings[k].finish_near()
    for at in ((x + 3) % NX, (x + 1) % NX):
        f_core.append(w.go(f_line(at), f_line(at), core))
    e_core = spread_rest(lambda: None)
    for k in range(NZ):
        rings[k].finish_far()
    f_core.append(w.go(f_line((x + 2) % NX), f_line((x + 2) % NX), core))
    for copy in f_core:
        copy.wait_recv()
    firsts = pl.ds(0, OWNERS)
    store(all_of.at[firsts], all_out.at[firsts])
    for copy in e_core:
        copy.wait_recv()
    extras = pl.ds(OWNERS, EXTRAS)
    store(all_of.at[extras], all_out.at[extras])

    for copy in stores:
        copy.wait()
    for copy in w.sent:
        copy.wait_send()
    for here, copy in stat_copies + n_copies + t_copies:

        @pl.when(jnp.logical_not(here))
        def _():
            copy.wait_send()

    for s in range(SLOTS):

        @pl.when(j != 2 * s + c)
        def _():
            g_copies[s].wait_send()

    @pl.when(primary)
    def _():
        for copy in handed:
            copy.wait_send()

    @pl.when(c == 0)
    def _():
        for copy in h_copies:
            copy.wait_send()

    @pl.when(c == 1)
    def _():
        for i in range(NM):

            @pl.when(jnp.logical_not((zl == 1) & (j == i)))
            def _():
                d_copies[i].wait_send()


def whole_step(table, grads, left, right, first, second):
    state = jax.ShapeDtypeStruct((SLOTS, ROWS, COLS), F32)
    v = lambda *shape, kind=BF16: pltpu.VMEM(shape, kind)
    dma = pltpu.SemaphoreType.DMA
    half = (HALF, COLS)
    full = (ROWS, COLS)
    return pl.pallas_call(
        kernel,
        out_shape=(jax.ShapeDtypeStruct((BLOCKS, ROWS, COLS), BF16), state, state, state, state),
        in_specs=[SMEM] + [ANY] * 5,
        out_specs=(ANY,) * 5,
        scratch_shapes=[v(BLOCKS, *full)]
        + [v(SLOTS, *full, kind=F32)] * 4
        + [v(BLOCKS, *full)]
        + [v(SLOTS, *full, kind=F32)] * 4
        + [
            v(NK, *full), v(NK, *half), v(NK, *full), v(NK, *half), v(NK, *full), v(NK, *half),
            v(2, 2, *full), v(2, 2, *half), v(2, NZ, *full), v(2, NZ, *half), v(NZ, *full), v(NZ, *half),
            v(3, *full), v(3, *half), v(EXTRAS, *full), v(SLOTS, *full),
        ]
        + [
            v(ORDER, COLS), v(ORDER, COLS, kind=F32), v(SLOTS, 8, 128, kind=F32), v(NM, 8, 128, kind=F32),
            v(ORDER, COLS, kind=F32), v(ORDER, COLS), v(2, SLOTS, *full),
        ]
        + [v(ORDER, COLS)] * 7
        + [v(SLOTS, *full)]
        + [
            v(EXTRAS, *half), v(EXTRAS, *half), v(EXTRAS, *half), v(2, 2, *half),
            v(2, NZ, *half), v(NZ, *half), v(3, *half),
        ]
        + [dma((SEMS,)), dma((SEMS,)), dma((5,)), dma((7,))],
        compiler_params=pltpu.CompilerParams(
            collective_id=0, has_side_effects=True, vmem_limit_bytes=56 << 20
        ),
        name="shampoo_step",
    )(table, grads, left, right, first, second)


def table_kernel(owner, table, counts):
    me = lax.axis_index("dp")

    def clear(i, carry):
        table[i] = 0
        return carry

    def clear_counts(i, carry):
        counts[i] = 0
        return carry

    lax.fori_loop(OCCUPIED, MINE_OF + EXTRAS, clear, 0)
    lax.fori_loop(0, OWNERS, clear_counts, 0)

    def visit(b, rank):
        o = owner[b]
        slot = counts[o]
        counts[o] = slot + 1
        again = slot > 0
        table[jnp.where(again, OWNERS + rank, o)] = b
        table[PLACE_OF + b] = jnp.where(again, OWNERS + rank, (o % NC) * NK + o // NC)

        @pl.when(o == me)
        def _():
            table[OCCUPIED + slot] = 1

            @pl.when(again)
            def _():
                table[EXTRA_OF + slot] = rank
                table[MINE_OF + rank] = slot

        return rank + again.astype(jnp.int32)

    lax.fori_loop(0, BLOCKS, visit, jnp.int32(0))


def tables(owners):
    return pl.pallas_call(
        table_kernel,
        out_shape=jax.ShapeDtypeStruct((TABLE,), jnp.int32),
        in_specs=[SMEM],
        out_specs=SMEM,
        scratch_shapes=[pltpu.SMEM((OWNERS,), jnp.int32)],
        name="tables",
    )(owners[:, 0])


def output_kernel(
    table, all_of, a, b, c, d, out, a_out, b_out, c_out, d_out, held, a_held, b_held, c_held, d_held, came, sent
):
    load = pltpu.make_async_copy(all_of, held, came.at[0])
    load.start()
    states = ((a, a_held, a_out), (b, b_held, b_out), (c, c_held, c_out), (d, d_held, d_out))
    ins = [pltpu.make_async_copy(src, mid, came.at[1 + i]) for i, (src, mid, _) in enumerate(states)]
    outs = [pltpu.make_async_copy(mid, dst.at[0], sent.at[1 + i]) for i, (_, mid, dst) in enumerate(states)]
    for copy in ins:
        copy.start()
    load.wait()
    for i in range(BLOCKS):
        pltpu.make_async_copy(held.at[table[PLACE_OF + i]], out.at[i], sent.at[0]).start()
    for copy_in, copy_out in zip(ins, outs):
        copy_in.wait()
        copy_out.start()
    pltpu.make_async_copy(held, out, sent.at[0]).wait()
    for copy in outs:
        copy.wait()


def outputs(table, *parts):
    state = jax.ShapeDtypeStruct((1, SLOTS, ROWS, COLS), F32)
    return pl.pallas_call(
        output_kernel,
        out_shape=(jax.ShapeDtypeStruct((BLOCKS, ROWS, COLS), BF16), state, state, state, state),
        in_specs=[SMEM] + [ANY] * 5,
        out_specs=(ANY,) * 5,
        scratch_shapes=[pltpu.VMEM((BLOCKS, ROWS, COLS), BF16)]
        + [pltpu.VMEM((SLOTS, ROWS, COLS), F32)] * 4
        + [pltpu.SemaphoreType.DMA((5,))] * 2,
        compiler_params=pltpu.CompilerParams(vmem_limit_bytes=56 << 20),
        name="outputs",
    )(table, *parts)


def body(grads, owners, left_stat, right_stat, first_moment, second_moment):
    table = tables(owners)
    parts = whole_step(table, grads[0], left_stat[0], right_stat[0], first_moment[0], second_moment[0])
    return outputs(table, *parts)


def solution(mesh):
    split = P("dp", None, "mp", None)
    return jax.shard_map(
        body,
        mesh=mesh,
        in_specs=(split, P(), split, split, split, split),
        out_specs=(P(None, "mp", None), split, split, split, split),
        check_vma=False,
    )
```

```python
import jax
import jax.numpy as jnp
from jax import lax
from jax.experimental import pallas as pl
from jax.experimental.pallas import tpu as pltpu
from jax.sharding import PartitionSpec as P

ITERS = 6
MESH = pl.DeviceIdType.MESH
VMEM = pl.BlockSpec(memory_space=pltpu.VMEM)
SMEM = pl.BlockSpec(memory_space=pltpu.SMEM)
ANY = pl.BlockSpec(memory_space=pl.ANY)
F32, BF16 = jnp.float32, jnp.bfloat16
NX, NZ, NC, NM = 4, 4, 2, 8
NK = NX * NZ
ROWS, COLS, HALF = 64, 512, 32
ORDER = NM * ROWS
SLOTS = 4
BLOCKS = 48
OWNERS = NK * NC
EXTRAS = BLOCKS - OWNERS
FAR_FIRST = (2, 1, 3)
SEMS = 256
PLACE_OF, OCCUPIED, EXTRA_OF, MINE_OF, TABLE = 48, 96, 100, 104, 128


def dp_of(x, z, c):
    return {"dp": (x * NZ + z) * NC + c}


def device_of(x, z, c, j):
    return {"dp": (x * NZ + z) * NC + c, "mp": j}


def total(*parts):
    value = parts[0].astype(F32)
    for part in parts[1:]:
        value = value + part.astype(F32)
    return value.astype(BF16)


def mm(a, b):
    return jnp.dot(a, b, preferred_element_type=F32)


class Wires:
    def __init__(self, send, recv):
        self.send, self.recv, self.used, self.sent = send, recv, 0, []

    def take(self, count):
        self.used += count
        assert self.used <= SEMS
        return self.used - count

    def make(self, src, dst, device, at_send, at_recv):
        return pltpu.make_async_remote_copy(
            src_ref=src, dst_ref=dst, send_sem=self.send.at[at_send], recv_sem=self.recv.at[at_recv],
            device_id=device, device_id_type=MESH,
        )

    def go(self, src, dst, device):
        at = self.take(1)
        copy = self.make(src, dst, device, at, at)
        copy.start()
        self.sent.append(copy)
        return copy


class RingReduce:
    def __init__(self, wires, acc, passed, came, x, to):
        self.wires, self.acc, self.passed, self.came, self.x, self.to = wires, acc, passed, came, x, to
        self.right, self.left, self.far = (x + 1) % NX, (x + 3) % NX, (x + 2) % NX

    def part(self, at, h):
        return self.acc.at[pl.ds(at * NZ + 2 * h, 2)]

    def send_far(self):
        self.a = self.wires.go(self.part(self.far, 0), self.passed.at[0], self.to(self.right))
        self.b = self.wires.go(self.part(self.far, 1), self.passed.at[1], self.to(self.left))

    def send_right(self):
        self.c = self.wires.go(self.part(self.right, 1), self.came.at[0, pl.ds(2, 2)], self.to(self.right))

    def send_left(self):
        self.d = self.wires.go(self.part(self.left, 0), self.came.at[1, pl.ds(0, 2)], self.to(self.left))

    def forward(self):
        self.a.wait_recv()
        for q in range(2):
            at = self.right * NZ + q
            self.acc[at] = total(self.acc[at], self.passed[0, q])
        self.e = self.wires.go(self.part(self.right, 0), self.came.at[0, pl.ds(0, 2)], self.to(self.right))
        self.b.wait_recv()
        for q in range(2):
            at = self.left * NZ + 2 + q
            self.acc[at] = total(self.acc[at], self.passed[1, q])
        self.f = self.wires.go(self.part(self.left, 1), self.came.at[1, pl.ds(2, 2)], self.to(self.left))

    def finish(self, out):
        for copy in (self.c, self.d, self.e, self.f):
            copy.wait_recv()
        for q in range(NZ):
            out[q] = total(self.acc[self.x * NZ + q], self.came[0, q], self.came[1, q])


class RingGather:
    def __init__(self, wires, part, x, to):
        self.wires, self.part = wires, part
        self.x, self.right, self.left = x, (x + 1) % NX, (x + 3) % NX
        self.to_right, self.to_left = to(self.right), to(self.left)

    def push(self, at, h, device):
        return self.wires.go(self.part(at, h), self.part(at, h), device)

    def start(self):
        self.a = self.push(self.x, 0, self.to_right)
        self.b = self.push(self.x, 1, self.to_left)
        self.c = self.push(self.x, 1, self.to_right)
        self.d = self.push(self.x, 0, self.to_left)

    def forward(self):
        self.a.wait_recv()
        self.e = self.push(self.left, 0, self.to_right)
        self.b.wait_recv()
        self.f = self.push(self.right, 1, self.to_left)

    def finish_near(self):
        self.c.wait_recv()
        self.d.wait_recv()

    def finish_far(self):
        self.e.wait_recv()
        self.f.wait_recv()


def kernel(
    table, grads, left, right, first, second,
    all_out, left_hbm, right_hbm, first_hbm, second_hbm,
    gv, lv, rv, fv, sv, all_of, left_out, right_out, first_out, second_out,
    send_f, send_e, recv_f, recv_e, acc_f, acc_e, pass_f, pass_e, came_f, came_e, sum_f, sum_e,
    from_z_f, from_z_e, ext, own,
    grad, stat, norms, norms_in, mat, term, terms, power, factor, current, root, half, half_in, turned, update,
    send_d, recv_d, acc_d, pass_d, came_d, sum_d, from_z_d,
    send_sem, recv_sem, load_sem, store_sem,
):
    me = lax.axis_index("dp")
    j = lax.axis_index("mp")
    x, z, c = me // (NZ * NC), (me // NC) % NZ, me % NC
    y, zl = j // 2, j % 2
    other = 1 - c
    core = dp_of(x, z, other)
    to_x = lambda at: dp_of(at, z, c)
    w = Wires(send_sem, recv_sem)
    my_rows = pl.ds(j * ROWS, ROWS)
    lanes = lax.broadcasted_iota(jnp.int32, (ROWS, 128), 1)
    lines = lax.broadcasted_iota(jnp.int32, (ROWS, 128), 0)

    loads = [
        pltpu.make_async_copy(src, dst, load_sem.at[i])
        for i, (src, dst) in enumerate(((grads, gv), (left, lv), (right, rv), (first, fv), (second, sv)))
    ]
    for copy in loads:
        copy.start()

    barrier = pltpu.get_barrier_semaphore()
    greeted = 0
    for k in range(1, 4):
        for device in (dp_of((x + k) % NX, z, c), dp_of(x, (z + k) % NZ, c)):
            pl.semaphore_signal(barrier, inc=1, device_id=device, device_id_type=MESH)
            greeted += 1
    for k in range(NM):
        for which in range(NC):
            if k or which:
                device = device_of(x, z, (c + which) % NC, (j + k) % NM)
                pl.semaphore_signal(barrier, inc=1, device_id=device, device_id_type=MESH)
                greeted += 1
    pl.semaphore_wait(barrier, greeted)

    stat_send, stat_recv = w.take(2 * SLOTS), w.take(NM)
    stat_copies = []
    for s in range(SLOTS):
        for role, source in enumerate((left, right)):
            copy = w.make(
                source.at[s], stat.at[my_rows], device_of(x, z, role, 2 * s + c), stat_send + 2 * s + role,
                stat_recv + j,
            )
            here = (c == role) & (j == 2 * s + c)
            stat_copies.append((here, copy))

    def send_stats(role):
        for here, copy in stat_copies[role::NC]:

            @pl.when(jnp.logical_not(here))
            def _():
                copy.start()

    send_stats(0)

    loads[0].wait()
    for k in range(NK):
        send_e[k] = gv[table[OWNERS + k], pl.ds(other * HALF, HALF)]
    core_e = w.go(send_e, recv_e, core)
    turns = (2, 1, 3, 0)
    core_f = []
    for k in turns:
        at = (x + k) % NX
        for q in range(NZ):
            send_f[at * NZ + q] = gv[table[(at * NZ + q) * NC + other]]
        rows = pl.ds(at * NZ, NZ)
        core_f.append(w.go(send_f.at[rows], recv_f.at[rows], core))

    ring_e = RingReduce(w, acc_e, pass_e, came_e, x, to_x)
    ring_f = RingReduce(w, acc_f, pass_f, came_f, x, to_x)
    core_e.wait_recv()

    def add_e(step):
        for q in range(NZ):
            k = ((x + turns[step]) % NX) * NZ + q
            acc_e[k] = total(gv[table[OWNERS + k], pl.ds(c * HALF, HALF)], recv_e[k])

    add_e(0)
    ring_e.send_far()
    add_e(1)
    ring_e.send_right()
    add_e(2)
    ring_e.send_left()
    add_e(3)

    def add_f(step):
        at = (x + turns[step]) % NX
        core_f[step].wait_recv()
        for q in range(NZ):
            acc_f[at * NZ + q] = total(gv[table[(at * NZ + q) * NC + c]], recv_f[at * NZ + q])

    loads[1].wait()
    loads[2].wait()
    for s in range(SLOTS):
        for role, source in enumerate((lv, rv)):

            @pl.when((c == role) & (j == 2 * s + c))
            def _():
                stat[my_rows] = source[s]

    add_f(0)
    ring_e.forward()
    ring_f.send_far()
    add_f(1)
    ring_f.send_right()
    add_f(2)
    ring_f.send_left()
    add_f(3)
    ring_e.finish(sum_e)
    z_e = [w.go(sum_e.at[(z + k) % NZ], from_z_e.at[k - 1], dp_of(x, (z + k) % NZ, c)) for k in FAR_FIRST]
    ring_f.forward()
    for copy in z_e:
        copy.wait_recv()
    mine = ext.at[x * NZ + z, pl.ds(c * HALF, HALF)]
    ext[x * NZ + z, pl.ds(c * HALF, HALF)] = total(sum_e[z], from_z_e[0], from_z_e[1], from_z_e[2])
    z_g = [w.go(mine, mine, dp_of(x, (z + k) % NZ, c)) for k in FAR_FIRST]

    def spread(ref, base, zs):
        def ring_of(k):
            at_z = (z + NZ - k) % NZ
            part = lambda at, h: ref.at[base + at * NZ + at_z, pl.ds(c * HALF + h * 16, 16)]
            return RingGather(w, part, x, to_x)

        line = lambda at: ref.at[pl.ds(base + at * NZ, NZ), pl.ds(c * HALF, HALF)]
        rings = {k: ring_of(k) for k in range(NZ)}
        rings[0].start()

        def rest(meanwhile):
            for k in (1, 3, 2):
                zs[FAR_FIRST.index(k)].wait_recv()
                rings[k].start()
            across = [w.go(line(x), line(x), core)]
            meanwhile()
            for k in (0, 1, 3, 2):
                rings[k].forward()
            for k in range(NZ):
                rings[k].finish_near()
            for at in ((x + 3) % NX, (x + 1) % NX):
                across.append(w.go(line(at), line(at), core))
            for k in range(NZ):
                rings[k].finish_far()
            far = (x + 2) % NX
            across.append(w.go(line(far), line(far), core))
            return across

        return rest

    spread_rest = spread(ext, 0, z_g)
    ring_f.finish(sum_f)
    z_f = [w.go(sum_f.at[(z + k) % NZ], from_z_f.at[k - 1], dp_of(x, (z + k) % NZ, c)) for k in FAR_FIRST]
    ext_core = spread_rest(lambda: send_stats(1))
    for copy in z_f:
        copy.wait_recv()
    own[0] = total(sum_f[z], from_z_f[0], from_z_f[1], from_z_f[2])

    g_send, g_recv, g_core = w.take(SLOTS), w.take(NM), w.take(NM)
    g_copies = [
        w.make(own.at[s], grad.at[my_rows], {"mp": 2 * s + c}, g_send + s, g_recv + j) for s in range(SLOTS)
    ]
    primary = c == zl

    def send_g(s):
        @pl.when(j != 2 * s + c)
        def _():
            g_copies[s].start()

        @pl.when(j == 2 * s + c)
        def _():
            grad[my_rows] = own[s]

    send_g(0)
    for copy in ext_core:
        copy.wait_recv()
    for s in range(1, SLOTS):
        own[s] = ext[table[EXTRA_OF + s]]
        send_g(s)

    stores = []

    def store(src, dst):
        copy = pltpu.make_async_copy(src, dst, store_sem.at[len(stores)])
        copy.start()
        stores.append(copy)

    loads[3].wait()
    loads[4].wait()
    n_send, n_recv = w.take(SLOTS), w.take(NM)
    n_copies = []
    for s in range(SLOTS):
        held = jnp.full((ROWS, COLS), table[OCCUPIED + s]) > 0
        g = own[s].astype(F32)
        m = 0.9 * fv[s] + 0.1 * g
        v = 0.95 * sv[s] + 0.05 * g * g
        first_out[s] = jnp.where(held, m, fv[s])
        second_out[s] = jnp.where(held, v, sv[s])
        a = m / (jnp.sqrt(v) + 1e-8)
        length = jnp.broadcast_to(jnp.sqrt(jnp.sum(a * a, axis=1, keepdims=True)), (ROWS, 128))
        length = jnp.sum(jnp.where(lanes == lines, length, 0.0), axis=0, keepdims=True)
        norms[s] = jnp.broadcast_to(length, (8, 128))
        copy = w.make(norms.at[s], norms_in.at[j], device_of(x, z, 1, 2 * s + c), n_send + s, n_recv + j)
        here = (c == 1) & (j == 2 * s + c)
        n_copies.append((here, copy))

        @pl.when(jnp.logical_not(here))
        def _():
            copy.start()

        @pl.when(here)
        def _():
            norms_in[j] = norms[s]

    store(first_out, first_hbm)
    store(second_out, second_hbm)
    handed = [
        w.make(grad.at[pl.ds(i * ROWS, ROWS)], grad.at[pl.ds(i * ROWS, ROWS)], core, g_core + i, g_core + i)
        for i in range(NM)
    ]

    @pl.when(primary)
    def _():
        for i in range(NM):

            @pl.when(j != i)
            def _():
                w.make(own.at[0], grad.at[pl.ds(i * ROWS, ROWS)], core, g_send, g_recv + i).wait_recv()

            handed[i].start()

    @pl.when(jnp.logical_not(primary))
    def _():
        for i in range(NM):
            handed[i].wait_recv()

    @pl.when(c == 0)
    def _():
        g = grad[...]
        mat[...] = lax.dot_general(g, g, (((1,), (1,)), ((), ())), preferred_element_type=F32)

    @pl.when(c == 1)
    def _():
        g = grad[...]
        mat[...] = lax.dot_general(g, g, (((0,), (0,)), ((), ())), preferred_element_type=F32)

    for i in range(NM):

        @pl.when(jnp.logical_not((zl == c) & (j == i)))
        def _():
            w.make(lv.at[0], stat.at[pl.ds(i * ROWS, ROWS)], core, stat_send, stat_recv + i).wait_recv()

    term[...] = mat[...].astype(BF16)
    t_send, t_recv = w.take(NM), w.take(2 * SLOTS)
    t_copies = []
    for i in range(NM):
        copy = w.make(
            term.at[pl.ds(i * ROWS, ROWS)], terms.at[c, y], device_of(x, z, zl, i), t_send + i,
            t_recv + c * SLOTS + y,
        )
        here = (zl == c) & (j == i)
        t_copies.append((here, copy))

        @pl.when(jnp.logical_not(here))
        def _():
            copy.start()

        @pl.when(here)
        def _():
            terms[c, y] = term[pl.ds(i * ROWS, ROWS)]

    whole = 0.9 * stat[...] + 0.1 * mat[...]
    mat[...] = whole
    frobenius = jnp.sqrt(jnp.sum(whole * whole, keepdims=True))
    scaling = 5.0 / (2.0 * frobenius)
    start = jnp.sqrt(jnp.sqrt(scaling)).astype(BF16).astype(F32)
    diagonal = lax.broadcasted_iota(jnp.int32, (ORDER, ORDER), 0) == lax.broadcasted_iota(
        jnp.int32, (ORDER, ORDER), 1
    )
    five = jnp.where(diagonal, 5.0, 0.0).astype(F32)
    current[...] = (scaling * mat[...]).astype(BF16)
    factor[...] = ((five - current[...].astype(F32)) * 0.25).astype(BF16)
    root[...] = (start * factor[...].astype(F32)).astype(BF16)

    def sweep(_, carry):
        power[...] = mm(factor[...], factor[...]).astype(BF16)
        power[...] = mm(power[...], power[...]).astype(BF16)
        current[...] = mm(power[...], current[...]).astype(BF16)
        factor[...] = ((five - current[...].astype(F32)) * 0.25).astype(BF16)
        root[...] = mm(root[...], factor[...]).astype(BF16)
        return carry

    lax.fori_loop(0, ITERS - 1, sweep, 0)

    step = 2 * ROWS
    count = ORDER // step
    h_at = w.take(count)
    h_copies = [
        w.make(half.at[pl.ds(i * step, step)], half_in.at[pl.ds(i * step, step)], core, h_at + i, h_at + i)
        for i in range(count)
    ]
    d_send, d_recv = w.take(NM), w.take(SLOTS)
    d_copies = [
        w.make(
            turned.at[pl.ds(i * ROWS, ROWS)], update.at[y], device_of(x, z, zl, i), d_send + i, d_recv + y
        )
        for i in range(NM)
    ]

    @pl.when(c == 0)
    def _():
        for i in range(count):
            rows = pl.ds(i * step, step)
            half[rows] = mm(root[rows], grad[...]).astype(BF16)
            h_copies[i].start()

    @pl.when(c == 1)
    def _():
        for i in range(NM):

            @pl.when(jnp.logical_not((zl == 1) & (j == i)))
            def _():
                w.make(norms.at[0], norms_in.at[i], core, n_send, n_recv + i).wait_recv()

        for i in range(count):
            rows = pl.ds(i * step, step)
            h_copies[i].wait_recv()
            s = mm(half_in[rows], root[...])
            for u in range(2):
                to = 2 * i + u
                here = (zl == 1) & (j == to)
                piece = s[u * ROWS : (u + 1) * ROWS]
                length = jnp.sqrt(jnp.sum(piece * piece, axis=1, keepdims=True)) + 1e-6
                adam = jnp.broadcast_to(norms_in[to, 0:1], (ROWS, 128))
                adam = jnp.sum(jnp.where(lanes == lines, adam, 0.0), axis=1, keepdims=True)
                turned[pl.ds(to * ROWS, ROWS)] = (piece * (adam / length)).astype(BF16)

                @pl.when(jnp.logical_not(here))
                def _():
                    d_copies[to].start()

                @pl.when(here)
                def _():
                    update[y] = turned[pl.ds(to * ROWS, ROWS)]

    def wait_update(s):
        @pl.when(jnp.logical_not((c == 1) & (j == 2 * s + c)))
        def _():
            w.make(turned.at[pl.ds(0, ROWS)], update.at[s], core, d_send, d_recv + s).wait_recv()

    here_f = c * NK + x * NZ + z
    wait_update(0)
    all_of[here_f] = update[0]
    f_z = [w.go(all_of.at[here_f], all_of.at[here_f], dp_of(x, (z + k) % NZ, c)) for k in FAR_FIRST]

    def ring_of(k):
        at_z = (z + NZ - k) % NZ
        part = lambda at, h: all_of.at[c * NK + at * NZ + at_z, pl.ds(h * HALF, HALF)]
        return RingGather(w, part, x, to_x)

    rings = {k: ring_of(k) for k in range(NZ)}
    for q in range(1, SLOTS):
        wait_update(q)

    def picked(e, which):
        at = table[MINE_OF + e]
        value = update[at, pl.ds(which * HALF, HALF)]
        return jnp.where(jnp.full(value.shape, at) > 0, value.astype(F32), 0.0)

    for e in range(EXTRAS):
        send_d[e] = picked(e, other).astype(BF16)
    core_d = w.go(send_d, recv_d, core)
    ring_d = RingReduce(w, acc_d, pass_d, came_d, x, to_x)
    core_d.wait_recv()
    for k, send in ((2, ring_d.send_far), (1, ring_d.send_right), (3, ring_d.send_left), (0, None)):
        for q in range(NZ):
            e = ((x + k) % NX) * NZ + q
            acc_d[e] = (picked(e, c) + recv_d[e].astype(F32)).astype(BF16)
        if send:
            send()
    ring_d.forward()
    rings[0].start()
    ring_d.finish(sum_d)
    z_d = [w.go(sum_d.at[(z + k) % NZ], from_z_d.at[k - 1], dp_of(x, (z + k) % NZ, c)) for k in FAR_FIRST]
    for copy, k in sorted(zip(f_z, FAR_FIRST), key=lambda pair: pair[1] == 2):
        copy.wait_recv()
        rings[k].start()
    f_line = lambda at: all_of.at[pl.ds(c * NK + at * NZ, NZ)]
    f_core = [w.go(f_line(x), f_line(x), core)]
    rings[0].forward()
    for copy in z_d:
        copy.wait_recv()
    here_e = (OWNERS + x * NZ + z, pl.ds(c * HALF, HALF))
    all_of[here_e] = total(sum_d[z], from_z_d[0], from_z_d[1], from_z_d[2])
    mine = all_of.at[here_e]
    z_g = [w.go(mine, mine, dp_of(x, (z + k) % NZ, c)) for k in FAR_FIRST]
    spread_rest = spread(all_of, OWNERS, z_g)
    for k in (1, 3, 2):
        rings[k].forward()

    for role in range(2):
        for s in range(SLOTS):

            @pl.when(jnp.logical_not((role == c) & (j == 2 * s + c)))
            def _():
                w.make(
                    term.at[pl.ds(0, ROWS)], terms.at[role, s], core, t_send, t_recv + role * SLOTS + s
                ).wait_recv()

            old, new = ((lv, left_out), (rv, right_out))[role]
            held = jnp.full((ROWS, COLS), table[OCCUPIED + s]) > 0
            new[s] = jnp.where(held, 0.9 * old[s] + 0.1 * terms[role, s].astype(F32), old[s])

    store(left_out, left_hbm)
    store(right_out, right_hbm)
    for k in range(NZ):
        rings[k].finish_near()
    for at in ((x + 3) % NX, (x + 1) % NX):
        f_core.append(w.go(f_line(at), f_line(at), core))
    e_core = spread_rest(lambda: None)
    for k in range(NZ):
        rings[k].finish_far()
    f_core.append(w.go(f_line((x + 2) % NX), f_line((x + 2) % NX), core))
    for copy in f_core:
        copy.wait_recv()
    firsts = pl.ds(0, OWNERS)
    store(all_of.at[firsts], all_out.at[firsts])
    for copy in e_core:
        copy.wait_recv()
    extras = pl.ds(OWNERS, EXTRAS)
    store(all_of.at[extras], all_out.at[extras])

    for copy in stores:
        copy.wait()
    for copy in w.sent:
        copy.wait_send()
    for here, copy in stat_copies + n_copies + t_copies:

        @pl.when(jnp.logical_not(here))
        def _():
            copy.wait_send()

    for s in range(SLOTS):

        @pl.when(j != 2 * s + c)
        def _():
            g_copies[s].wait_send()

    @pl.when(primary)
    def _():
        for copy in handed:
            copy.wait_send()

    @pl.when(c == 0)
    def _():
        for copy in h_copies:
            copy.wait_send()

    @pl.when(c == 1)
    def _():
        for i in range(NM):

            @pl.when(jnp.logical_not((zl == 1) & (j == i)))
            def _():
                d_copies[i].wait_send()


def whole_step(table, grads, left, right, first, second):
    state = jax.ShapeDtypeStruct((SLOTS, ROWS, COLS), F32)
    v = lambda *shape, kind=BF16: pltpu.VMEM(shape, kind)
    dma = pltpu.SemaphoreType.DMA
    half = (HALF, COLS)
    full = (ROWS, COLS)
    return pl.pallas_call(
        kernel,
        out_shape=(jax.ShapeDtypeStruct((BLOCKS, ROWS, COLS), BF16), state, state, state, state),
        in_specs=[SMEM] + [ANY] * 5,
        out_specs=(ANY,) * 5,
        scratch_shapes=[v(BLOCKS, *full)]
        + [v(SLOTS, *full, kind=F32)] * 4
        + [v(BLOCKS, *full)]
        + [v(SLOTS, *full, kind=F32)] * 4
        + [
            v(NK, *full), v(NK, *half), v(NK, *full), v(NK, *half), v(NK, *full), v(NK, *half),
            v(2, 2, *full), v(2, 2, *half), v(2, NZ, *full), v(2, NZ, *half), v(NZ, *full), v(NZ, *half),
            v(3, *full), v(3, *half), v(EXTRAS, *full), v(SLOTS, *full),
        ]
        + [
            v(ORDER, COLS), v(ORDER, COLS, kind=F32), v(SLOTS, 8, 128, kind=F32), v(NM, 8, 128, kind=F32),
            v(ORDER, COLS, kind=F32), v(ORDER, COLS), v(2, SLOTS, *full),
        ]
        + [v(ORDER, COLS)] * 7
        + [v(SLOTS, *full)]
        + [
            v(EXTRAS, *half), v(EXTRAS, *half), v(EXTRAS, *half), v(2, 2, *half),
            v(2, NZ, *half), v(NZ, *half), v(3, *half),
        ]
        + [dma((SEMS,)), dma((SEMS,)), dma((5,)), dma((7,))],
        compiler_params=pltpu.CompilerParams(
            collective_id=0, has_side_effects=True, vmem_limit_bytes=56 << 20
        ),
        name="shampoo_step",
    )(table, grads, left, right, first, second)


def table_kernel(owner, table, counts):
    me = lax.axis_index("dp")

    def clear(i, carry):
        table[i] = 0
        return carry

    def clear_counts(i, carry):
        counts[i] = 0
        return carry

    lax.fori_loop(OCCUPIED, MINE_OF + EXTRAS, clear, 0)
    lax.fori_loop(0, OWNERS, clear_counts, 0)

    def visit(b, rank):
        o = owner[b]
        slot = counts[o]
        counts[o] = slot + 1
        again = slot > 0
        table[jnp.where(again, OWNERS + rank, o)] = b
        table[PLACE_OF + b] = jnp.where(again, OWNERS + rank, (o % NC) * NK + o // NC)

        @pl.when(o == me)
        def _():
            table[OCCUPIED + slot] = 1

            @pl.when(again)
            def _():
                table[EXTRA_OF + slot] = rank
                table[MINE_OF + rank] = slot

        return rank + again.astype(jnp.int32)

    lax.fori_loop(0, BLOCKS, visit, jnp.int32(0))


def tables(owners):
    return pl.pallas_call(
        table_kernel,
        out_shape=jax.ShapeDtypeStruct((TABLE,), jnp.int32),
        in_specs=[SMEM],
        out_specs=SMEM,
        scratch_shapes=[pltpu.SMEM((OWNERS,), jnp.int32)],
        name="tables",
    )(owners[:, 0])


def output_kernel(
    table, all_of, a, b, c, d, out, a_out, b_out, c_out, d_out, held, a_held, b_held, c_held, d_held, came, sent
):
    load = pltpu.make_async_copy(all_of, held, came.at[0])
    load.start()
    states = ((a, a_held, a_out), (b, b_held, b_out), (c, c_held, c_out), (d, d_held, d_out))
    ins = [pltpu.make_async_copy(src, mid, came.at[1 + i]) for i, (src, mid, _) in enumerate(states)]
    outs = [pltpu.make_async_copy(mid, dst.at[0], sent.at[1 + i]) for i, (_, mid, dst) in enumerate(states)]
    for copy in ins:
        copy.start()
    load.wait()
    for i in range(BLOCKS):
        pltpu.make_async_copy(held.at[table[PLACE_OF + i]], out.at[i], sent.at[0]).start()
    for copy_in, copy_out in zip(ins, outs):
        copy_in.wait()
        copy_out.start()
    pltpu.make_async_copy(held, out, sent.at[0]).wait()
    for copy in outs:
        copy.wait()


def outputs(table, *parts):
    state = jax.ShapeDtypeStruct((1, SLOTS, ROWS, COLS), F32)
    return pl.pallas_call(
        output_kernel,
        out_shape=(jax.ShapeDtypeStruct((BLOCKS, ROWS, COLS), BF16), state, state, state, state),
        in_specs=[SMEM] + [ANY] * 5,
        out_specs=(ANY,) * 5,
        scratch_shapes=[pltpu.VMEM((BLOCKS, ROWS, COLS), BF16)]
        + [pltpu.VMEM((SLOTS, ROWS, COLS), F32)] * 4
        + [pltpu.SemaphoreType.DMA((5,))] * 2,
        compiler_params=pltpu.CompilerParams(vmem_limit_bytes=56 << 20),
        name="outputs",
    )(table, *parts)


def body(grads, owners, left_stat, right_stat, first_moment, second_moment):
    table = tables(owners)
    parts = whole_step(table, grads[0], left_stat[0], right_stat[0], first_moment[0], second_moment[0])
    return outputs(table, *parts)


def solution(mesh):
    split = P("dp", None, "mp", None)
    return jax.shard_map(
        body,
        mesh=mesh,
        in_specs=(split, P(), split, split, split, split),
        out_specs=(P(None, "mp", None), split, split, split, split),
        check_vma=False,
    )
```
